128 devices in a mesh: gx: 8 (over y, x_lo), gy: 16 (over z, x_hi, core).
Axes of the slice: x: 4 (x_hi: 2, x_lo: 2; x = x_hi * 2 + x_lo), y: 4, z: 4, core: 2. Of those that a mesh axis runs over, the one named last changes fastest.
Arguments:
- electric: float32 [3, 128, 512, 128], P(None, 'gx', 'gy'), may hold values from -6 to 6
- magnetic: float32 [3, 128, 512, 128], P(None, 'gx', 'gy'), may hold values from -6 to 6
- material_ids: int32 [128, 512, 128], P('gx', 'gy'), may hold values from 0 to 7
- material_table: float32 [8, 9], replicated, as said below
Outputs:
- electric_out: float32 [3, 128, 512, 128], P(None, 'gx', 'gy')
- magnetic_out: float32 [3, 128, 512, 128], P(None, 'gx', 'gy')
The draws below stay inside these ranges and needn't reach their ends.
Inputs may be any that keep to these rules, and one draw needn't show every extreme that they name: `material_table`: each material's tensor is symmetric with diagonal entries above twice the sum of its off-diagonal magnitudes.
All inputs are finite; a program needn't handle non-finite values.
Results may differ from the reference program's by a relative error of at most 0.00002.
Values sent between devices are 32-bit elements; how exact they have to be, the bound alone decides.
A program may use at most 64 MiB of HBM per device.

```python
import jax
import jax.numpy as jnp

NZ = 128
STEPS = 12
MATS = 8
NX = 128
NY = 512


def draw_material_table(key, part):
    key = jax.random.fold_in(key, 11)
    keys = jax.random.split(key, 3)
    diag = jnp.exp(jax.random.uniform(keys[0], (MATS, 3), jnp.float32, jnp.log(0.45), 0.0))
    off = jax.random.uniform(keys[1], (MATS, 3), jnp.float32, -0.1, 0.1)
    source = jax.random.uniform(keys[2], (MATS, 3), jnp.float32, -1.5, 1.5)
    return jnp.concatenate([diag, off, source], axis=1)


def set_ends(entries, own_key, low, top_value):
    longest = entries.shape.index(max(entries.shape))
    spots = []
    for shift in (0, 1):
        where = [jax.random.randint(jax.random.fold_in(own_key, axis), (), 0, length) for axis, length in enumerate(entries.shape)]
        where[longest] = (where[longest] + shift) % entries.shape[longest]
        spots.append(tuple(where))
    return entries.at[spots[0]].set(low).at[spots[1]].set(top_value)


def levels(rng, shape, cuts, smallest, top_value):
    factor_of = 1.0
    for axis_at, parts in cuts:
        steps = jax.random.uniform(jax.random.fold_in(jax.random.fold_in(rng, 6), axis_at), (parts,), jnp.float32, smallest / len(cuts), top_value / len(cuts))
        factor_of = factor_of * jnp.repeat(jnp.exp(steps), shape[axis_at] // parts).reshape((-1,) + (1,) * (len(shape) - 1 - axis_at))
    return factor_of


def noise(own_key, extent, width, limit, shards=(), kind=jnp.bfloat16):
    gain = levels(own_key, extent, shards, -0.22, 0.18) if shards else 1.0
    entries = jax.random.normal(own_key, extent, jnp.float32) * width * gain
    return jnp.minimum(jnp.maximum(entries, -limit), limit).astype(kind)


def setup_inputs(seed: int = 0) -> dict:
    splits = jax.random.split(jax.random.key(seed), 5)
    return {
        "electric": noise(splits[0], (3, NX, NY, NZ), 1.0, 6.0, ((1, 8), (2, 16)), jnp.float32),
        "magnetic": noise(splits[1], (3, NX, NY, NZ), 1.0, 6.0, ((1, 8), (2, 16)), jnp.float32),
        "material_ids": set_ends(jax.random.randint(splits[2], (NX, NY, NZ), 0, MATS), jax.random.fold_in(splits[2], 1), 0, MATS - 1).astype(jnp.int32),
        "material_table": draw_material_table(jax.random.fold_in(splits[4], 71), 0),
    }


def shift_up(a, axis):
    zero = jnp.zeros_like(lax_slice(a, axis, 0, 1))
    return jnp.concatenate([lax_slice(a, axis, 1, a.shape[axis]), zero], axis=axis)


def shift_down(a, axis):
    zero = jnp.zeros_like(lax_slice(a, axis, 0, 1))
    return jnp.concatenate([zero, lax_slice(a, axis, 0, a.shape[axis] - 1)], axis=axis)


def lax_slice(a, axis, start, stop):
    index = [slice(None)] * a.ndim
    index[axis] = slice(start, stop)
    return a[tuple(index)]


def curl_forward(field):
    def diff(a, axis):
        return shift_up(a, axis) - a
    return jnp.stack([diff(field[2], 1) - diff(field[1], 2),
                      diff(field[0], 2) - diff(field[2], 0),
                      diff(field[1], 0) - diff(field[0], 1)])


def curl_backward(field):
    def diff(a, axis):
        return a - shift_down(a, axis)
    return jnp.stack([diff(field[2], 1) - diff(field[1], 2),
                      diff(field[0], 2) - diff(field[2], 0),
                      diff(field[1], 0) - diff(field[0], 1)])


def apply_tensor(coeff, vec):
    out_x = coeff[0] * vec[0] + coeff[3] * vec[1] + coeff[4] * vec[2]
    out_y = coeff[3] * vec[0] + coeff[1] * vec[1] + coeff[5] * vec[2]
    out_z = coeff[4] * vec[0] + coeff[5] * vec[1] + coeff[2] * vec[2]
    return jnp.stack([out_x, out_y, out_z])


def reference(electric, magnetic, material_ids, material_table):
    coeff = jnp.moveaxis(jnp.take(material_table, material_ids, axis=0), -1, 0)
    for step in range(STEPS):
        magnetic = magnetic - 0.45 * curl_forward(electric)
        amp = jnp.sin(jnp.float32(0.3 * (step + 1)))
        drive = curl_backward(magnetic) - amp * coeff[6:9]
        electric = electric + 0.45 * apply_tensor(coeff, drive)
    return electric, magnetic
```

```python
import functools

import jax
import jax.numpy as jnp
import numpy as np
from jax import lax
from jax.experimental import pallas as pl
from jax.experimental.pallas import tpu as pltpu
from jax.sharding import PartitionSpec as P

STEPS = 12
MATS = 8
BLOCK = 4
MESH = pl.DeviceIdType.MESH
NX, NY, NZ = 16, 32, 128
PX = BLOCK + 1
PY = 16
XP, YP = NX + 2 * PX, NY + 2 * PY
DEEP = BLOCK
MSGS = BLOCK + 1
FREE_PLANES = 13
BLOCKS = STEPS // BLOCK
SLOTS = BLOCKS * MSGS
DIRS = ((-1, 0), (1, 0), (0, -1), (0, 1), (-1, 1), (1, 1), (-1, -1), (1, -1))
W, E, S, N, NW, NE, SW, SE = range(8)
OPPOSITE = (E, W, N, S, SE, SW, NE, NW)
TILES = (12, 12, 8, 8, 4, 4, 4, 4)
MID = (8, 8, 4, 4, 0, 0, 0, 0)


def after_z(a, lane):
    return jnp.where(lane < NZ - 1, pltpu.roll(a, NZ - 1, 2), 0.0)


def before_z(a, lane):
    return jnp.where(lane > 0, pltpu.roll(a, 1, 2), 0.0)


def update_h(e, h, x, planes, row, n):
    lane = lax.broadcasted_iota(jnp.int32, (planes, n, NZ), 2)
    xs, ahead, rows, up = pl.ds(x, planes), pl.ds(x + 1, planes), pl.ds(row, n), pl.ds(row + 1, n)
    e0, e1, e2 = (e[c, xs, rows] for c in range(3))
    c0 = (e[2, xs, up] - e2) - (after_z(e1, lane) - e1)
    c1 = (after_z(e0, lane) - e0) - (e[2, ahead, rows] - e2)
    c2 = (e[1, ahead, rows] - e1) - (e[0, xs, up] - e0)
    new = [h[c, xs, rows] - curl for c, curl in enumerate((c0, c1, c2))]
    for c in range(3):
        h[c, xs, rows] = new[c]


def update_e(e, h, k, j, amp, x, planes, row, n):
    lane = lax.broadcasted_iota(jnp.int32, (planes, n, NZ), 2)
    xs, behind, rows, down = pl.ds(x, planes), pl.ds(x - 1, planes), pl.ds(row, n), pl.ds(row - 1, n)
    krows = pl.ds(row - 8, n)
    h0, h1, h2 = (h[c, xs, rows] for c in range(3))
    c0 = (h2 - h[2, xs, down]) - (h1 - before_z(h1, lane))
    c1 = (h0 - before_z(h0, lane)) - (h2 - h[2, behind, rows])
    c2 = (h1 - h[1, behind, rows]) - (h0 - h[0, xs, down])
    xx, yy, zz, xy, xz, yz = (k[c, xs, krows] for c in range(6))
    new0 = e[0, xs, rows] + ((xx * c0 + xy * c1) + (xz * c2 - amp * j[0, xs, krows]))
    new1 = e[1, xs, rows] + ((xy * c0 + yy * c1) + (yz * c2 - amp * j[1, xs, krows]))
    new2 = e[2, xs, rows] + ((xz * c0 + yz * c1) + (zz * c2 - amp * j[2, xs, krows]))
    for c, new in enumerate((new0, new1, new2)):
        e[c, xs, rows] = new


def sweep(lo, hi, most, body):
    count = hi - lo
    parts = -(-count // most)
    while count % parts:
        parts += 1
    planes = count // parts
    if parts == 1:
        body(lo, planes)
    else:
        def one(i, c):
            body(lo + i * planes, planes)
            return c

        lax.fori_loop(0, parts, one, 0)


def kernel(e_in, m_in, ids_in, table, e_out, m_out, et, ht, ef, hf, kk, jj, ids, own_x, own_y, ring, amps, *rest):
    out, inn = rest[:8], rest[8:16]
    out_sem, in_sem, id_out, id_in = rest[16:]
    gx, gy = lax.axis_index("gx"), lax.axis_index("gy")
    last_x, last_y = lax.axis_size("gx") - 1, lax.axis_size("gy") - 1

    def there(d):
        dx, dy = DIRS[d]
        checks = []
        if dx:
            checks.append(gx > 0 if dx < 0 else gx < last_x)
        if dy:
            checks.append(gy > 0 if dy < 0 else gy < last_y)
        return functools.reduce(jnp.logical_and, checks)

    def device(d):
        return (gx + DIRS[d][0], gy + DIRS[d][1])

    for d in range(8):
        def clear(s, c, d=d):
            inn[d][s] = jnp.zeros((TILES[d], 8, NZ), jnp.float32)
            return c
        lax.fori_loop(0, SLOTS, clear, 0)

    def clear_planes(x, c):
        ids[x] = jnp.full((YP - 16, NZ), -1, jnp.int32)
        for a in (ef, hf):
            for comp in range(3):
                a[comp, x] = jnp.zeros((YP, NZ), jnp.float32)
        return c

    lax.fori_loop(0, XP, clear_planes, 0)

    def clear_source(x, c):
        for comp in range(3):
            jj[comp, x] = jnp.zeros((YP - 16, NZ), jnp.float32)
        return c

    lax.fori_loop(0, XP, clear_source, 0)
    for step in range(STEPS):
        amps[step] = np.float32(np.sin(np.float32(0.3 * (step + 1))))

    barrier = pltpu.get_barrier_semaphore()
    for d in range(8):
        @pl.when(there(d))
        def _(d=d):
            pl.semaphore_signal(barrier, inc=1, device_id=device(d), device_id_type=MESH)
    peers = sum(there(d).astype(jnp.int32) for d in range(8))
    pl.semaphore_wait(barrier, peers)

    def id_copy(d):
        dx, dy = DIRS[d]
        xs = pl.ds(0 if dx < 0 else NX - DEEP, DEEP) if dx else pl.ds(0, NX)
        ys = pl.ds(0 if dy < 0 else NY - 8, 8) if dy else pl.ds(0, NY)
        xd = pl.ds(PX + NX if dx < 0 else PX - DEEP, DEEP) if dx else pl.ds(PX, NX)
        yd = pl.ds(8 + NY if dy < 0 else 0, 8) if dy else pl.ds(8, NY)
        return pltpu.make_async_remote_copy(
            src_ref=ids_in.at[xs, ys],
            dst_ref=ids.at[xd, yd],
            send_sem=id_out.at[d],
            recv_sem=id_in.at[d],
            device_id=device(d),
            device_id_type=MESH,
        )

    for d in range(8):
        @pl.when(there(d))
        def _(d=d):
            id_copy(d).start()

    def parts(d, slot, first, last):
        mid, tiles = MID[d], TILES[d]
        pieces = []
        if mid and not (first and d in (E, N)) and not (last and d in (W, S)):
            pieces.append((0, pl.ds(0, mid), pl.ds(0, 8)))
        if not first and not (last and d == SW):
            pieces.append((1, pl.ds(mid, tiles - mid), pl.ds(0, DEEP)))
        return pieces

    def copies(d, slot, first, last):
        return [
            pltpu.make_async_remote_copy(
                src_ref=out[d].at[slot, ts, rows],
                dst_ref=inn[d].at[slot, ts, rows],
                send_sem=out_sem.at[d, which, slot],
                recv_sem=in_sem.at[d, which, slot],
                device_id=device(d),
                device_id_type=MESH,
            )
            for which, ts, rows in parts(d, slot, first, last)
        ]

    def send(slot, first=False, last=False):
        for d in range(8):
            if parts(d, slot, first, last):
                @pl.when(there(d))
                def _(d=d):
                    for copy in copies(d, slot, first, last):
                        copy.start()

    def receive(slot, first=False, last=False):
        for d in range(8):
            if parts(d, slot, first, last):
                @pl.when(there(OPPOSITE[d]))
                def _(d=d):
                    for copy in copies(d, slot, first, last):
                        copy.wait_recv()

    def sent(slot, first=False, last=False):
        for d in range(8):
            if parts(d, slot, first, last):
                @pl.when(there(d))
                def _(d=d):
                    for copy in copies(d, slot, first, last):
                        copy.wait_send()

    XA, XZ, YA, YZ = PX, PX + NX - 1, PY, PY + NY - 1

    def put_face(d, slot, at, a, comps, x):
        for i, c in enumerate(comps):
            out[d][slot, pl.ds(at + 4 * i, 4)] = a[c, x, pl.ds(YA, NY)].reshape(4, 8, NZ)

    def put_line(d, slot, at, a, comps, y):
        for i, c in enumerate(comps):
            out[d][slot, pl.ds(at + 2 * i, 2)] = a[c, pl.ds(XA, NX), y].reshape(2, 8, NZ)

    def put_piece_y(d, slot, at, a, x, top):
        for i, c in enumerate((1, 2)):
            out[d][slot, at + i] = a[c, x, pl.ds(YZ + 1 if top else YA - DEEP, 8)]

    def put_piece_x(d, slot, at, a, y, right):
        for i, c in enumerate((0, 2)):
            out[d][slot, at + i, pl.ds(0, DEEP)] = a[c, pl.ds(XZ + 1 if right else XA - DEEP, DEEP), y]

    def pack_e(slot, corners=True):
        put_face(W, slot, 0, ef, (1, 2), XA)
        put_line(S, slot, 0, ef, (0, 2), YA)
        for i, c in enumerate((1, 2)):
            own_x[slot, 2 + i] = ef[c, XZ + 1, pl.ds(YA, NY)]
        for i, c in enumerate((0, 2)):
            own_y[slot, 2 + i] = ef[c, pl.ds(XA, NX), YZ + 1]
        if corners:
            put_piece_x(W, slot, 10, ef, YZ + 1, False)
            put_piece_x(E, slot, 10, ef, YZ + 1, True)
            put_piece_y(S, slot, 6, ef, XZ + 1, False)
            put_piece_y(N, slot, 6, ef, XZ + 1, True)
            put_piece_y(NW, slot, 0, ef, XA, True)
            put_piece_y(SW, slot, 0, ef, XA, False)
            put_piece_x(SW, slot, 2, ef, YA, False)
            put_piece_x(SE, slot, 2, ef, YA, True)

    def pack_h(slot):
        put_face(E, slot, 0, hf, (1, 2), XZ)
        put_line(N, slot, 0, hf, (0, 2), YZ)
        for i, c in enumerate((1, 2)):
            own_x[slot, i] = hf[c, XA - 1, pl.ds(YA, NY)]
        for i, c in enumerate((0, 2)):
            own_y[slot, i] = hf[c, pl.ds(XA, NX), YA - 1]
        put_piece_x(W, slot, 8, hf, YA - 1, False)
        put_piece_x(E, slot, 8, hf, YA - 1, True)
        put_piece_y(S, slot, 4, hf, XA - 1, False)
        put_piece_y(N, slot, 4, hf, XA - 1, True)
        put_piece_x(NW, slot, 2, hf, YZ, False)
        put_piece_y(NE, slot, 0, hf, XZ, True)
        put_piece_x(NE, slot, 2, hf, YZ, True)
        put_piece_y(SE, slot, 0, hf, XZ, False)

    def ring_x(a, x, slot, own, face, low, high):
        for i, c in enumerate((1, 2)):
            d, at = face
            a[c, x, pl.ds(YA, NY)] = own_x[slot, own + i] + inn[d][slot, pl.ds(at + 4 * i, 4)].reshape(NY, NZ)
            for pieces, row in ((low, YA), (high, YA + NY - DEEP)):
                (d1, at1), (d2, at2) = pieces
                a[c, x, pl.ds(row, 8)] = a[c, x, pl.ds(row, 8)] + (inn[d1][slot, at1 + i] + inn[d2][slot, at2 + i])

    def ring_y(a, y, slot, own, face, low, high):
        for i, c in enumerate((0, 2)):
            d, at = face
            ring[pl.ds(0, NX)] = own_y[slot, own + i] + inn[d][slot, pl.ds(at + 2 * i, 2)].reshape(NX, NZ)
            for pieces, row in ((low, 0), (high, NX - DEEP)):
                (d1, at1), (d2, at2) = pieces
                ring[pl.ds(row, 8)] = ring[pl.ds(row, 8)] + (inn[d1][slot, at1 + i] + inn[d2][slot, at2 + i])
            a[c, pl.ds(XA, NX), y] = ring[pl.ds(0, NX)]

    def ring_e(slot):
        ring_x(et, XZ + 1, slot, 2, (W, 0), ((N, 6), (NW, 0)), ((S, 6), (SW, 0)))
        ring_y(et, YZ + 1, slot, 2, (S, 0), ((E, 10), (SE, 2)), ((W, 10), (SW, 2)))

    def ring_h(slot):
        ring_x(ht, XA - 1, slot, 0, (E, 0), ((N, 4), (NE, 0)), ((S, 4), (SE, 0)))
        ring_y(ht, YA - 1, slot, 0, (N, 0), ((E, 8), (NE, 2)), ((W, 8), (NW, 2)))

    def look(x, row, n, source):
        here = ids[x, pl.ds(row, n)]
        bits = [(here & (1 << b)) != 0 for b in range(3)]
        real = here >= 0

        def pick(c):
            level = [table[m, c] for m in range(MATS)]
            for b in range(3):
                level = [jnp.where(bits[b], level[2 * i + 1], level[2 * i]) for i in range(len(level) // 2)]
            return level[0]

        tensor = [jnp.where(real, 0.2025 * pick(c), 0.0) for c in range(6)]
        for c in range(6):
            kk[c, x, pl.ds(row, n)] = tensor[c]
        if source:
            xx, yy, zz, xy, xz, yz = tensor
            s0, s1, s2 = ((1 / 0.45) * pick(c) for c in (6, 7, 8))
            jj[0, x, pl.ds(row, n)] = xx * s0 + xy * s1 + xz * s2
            jj[1, x, pl.ds(row, n)] = xy * s0 + yy * s1 + yz * s2
            jj[2, x, pl.ds(row, n)] = xz * s0 + yz * s1 + zz * s2

    def load(x, c):
        ids[x + PX, pl.ds(8, NY)] = ids_in[x]
        for comp in range(3):
            et[comp, x + PX, pl.ds(PY, NY)] = e_in[comp, x]
            ht[comp, x + PX, pl.ds(PY, NY)] = m_in[comp, x] * (1 / 0.45)
        return c

    lax.fori_loop(0, NX, load, 0)
    def look_own(x, c):
        look(x, 8, NY, True)
        return c

    def look_rows(x, c):
        look(x, 0, 8, False)
        look(x, 8 + NY, 8, False)
        return c

    def look_planes(x, c):
        look(x, 0, NY + 16, False)
        return c

    def block(b, c):
        base = b * MSGS

        def copy_in(x, c):
            for comp in range(3):
                for a, t in ((ef, et), (hf, ht)):
                    a[comp, x, pl.ds(8, 8)] = jnp.zeros((8, NZ), jnp.float32)
                    a[comp, x, pl.ds(PY, NY)] = t[comp, x, pl.ds(PY, NY)]
                    a[comp, x, pl.ds(PY + NY, 8)] = jnp.zeros((8, NZ), jnp.float32)
            return c

        def zero_plane(x, c):
            for comp in range(3):
                for a in (ef, hf):
                    a[comp, x, pl.ds(8, NY + 16)] = jnp.zeros((NY + 16, NZ), jnp.float32)
            return c

        lax.fori_loop(PX, PX + NX, copy_in, 0)

        @pl.when(b > 0)
        def _():
            lax.fori_loop(0, PX, zero_plane, 0)
            lax.fori_loop(PX + NX, XP, zero_plane, 0)

        pack_e(base, corners=False)
        send(base, first=True)

        @pl.when(b == 0)
        def _():
            lax.fori_loop(PX, PX + NX, look_own, 0)
            for d in range(8):
                @pl.when(there(OPPOSITE[d]))
                def _(d=d):
                    id_copy(d).wait_recv()
            lax.fori_loop(PX, PX + NX, look_rows, 0)
            lax.fori_loop(PX - DEEP, PX, look_planes, 0)
            lax.fori_loop(PX + NX, PX + NX + DEEP, look_planes, 0)

        def free_h(lo, hi):
            sweep(lo, hi, FREE_PLANES, lambda x, planes: update_h(ef, hf, x, planes, 8, NY + 16))

            @pl.when(gx == 0)
            def _():
                for comp in range(3):
                    hf[comp, PX - 1, pl.ds(8, NY + 16)] = jnp.zeros((NY + 16, NZ), jnp.float32)

            @pl.when(gy == 0)
            def _():
                for comp in range(3):
                    hf[comp, pl.ds(lo, hi - lo), pl.ds(8, 8)] = jnp.zeros((hi - lo, 8, NZ), jnp.float32)

        def free(t, c):
            amp = amps[b * BLOCK + t - 1]
            lo, hi = PX - (BLOCK - 1), PX + NX + BLOCK - 1
            free_h(lo, hi)
            sweep(lo, hi, FREE_PLANES, lambda x, planes: update_e(ef, hf, kk, jj, amp, x, planes, 8, NY + 16))
            pack_e(base + t)
            pack_h(base + t)
            send(base + t)
            return c

        lax.fori_loop(1, BLOCK, free, 0)
        free_h(PX - BLOCK, PX + NX + BLOCK - 1)
        pack_h(base + BLOCK)
        send(base + BLOCK, last=True)

        receive(base, first=True)

        def true_step(t):
            amp = amps[b * BLOCK + t - 1]
            ring_e(base + t - 1)
            ring_h(base + t)

            update_h(et, ht, PX, NX, PY, NY)
            update_e(et, ht, kk, jj, amp, PX, NX, PY, NY)

        def true(t, c):
            receive(base + t)
            true_step(t)
            return c

        lax.fori_loop(1, BLOCK, true, 0)
        receive(base + BLOCK, last=True)
        true_step(BLOCK)
        return c

    lax.fori_loop(0, BLOCKS, block, 0)

    def store(x, c):
        for comp in range(3):
            e_out[comp, x] = et[comp, x + PX, pl.ds(PY, NY)]
            m_out[comp, x] = ht[comp, x + PX, pl.ds(PY, NY)] * 0.45
        return c

    lax.fori_loop(0, NX, store, 0)

    for d in range(8):
        @pl.when(there(d))
        def _(d=d):
            id_copy(d).wait_send()

    def drain(b, c):
        sent(b * MSGS, first=True)

        def one(t, c):
            sent(b * MSGS + t)
            return c

        lax.fori_loop(1, BLOCK, one, 0)
        sent(b * MSGS + BLOCK, last=True)
        return c

    lax.fori_loop(0, BLOCKS, drain, 0)


def shards(electric, magnetic, material_ids, material_table):
    field = jax.ShapeDtypeStruct((3, NX, NY, NZ), jnp.float32)
    vmem = pl.BlockSpec(memory_space=pltpu.VMEM)
    big = pltpu.VMEM((3, XP, YP, NZ), jnp.float32)
    messages = [pltpu.VMEM((SLOTS, TILES[d], 8, NZ), jnp.float32) for d in range(8)]
    return pl.pallas_call(
        kernel,
        out_shape=(field, field),
        in_specs=[vmem, vmem, vmem, pl.BlockSpec(memory_space=pltpu.SMEM)],
        out_specs=(vmem, vmem),
        scratch_shapes=[
            big,
            big,
            big,
            big,
            pltpu.VMEM((6, XP, YP - 16, NZ), jnp.float32),
            pltpu.VMEM((3, XP, YP - 16, NZ), jnp.float32),
            pltpu.VMEM((XP, YP - 16, NZ), jnp.int32),
            pltpu.VMEM((SLOTS, 4, NY, NZ), jnp.float32),
            pltpu.VMEM((SLOTS, 4, NX, NZ), jnp.float32),
            pltpu.VMEM((NX + 8, NZ), jnp.float32),
            pltpu.SMEM((STEPS,), jnp.float32),
            *messages,
            *messages,
            pltpu.SemaphoreType.DMA((8, 2, SLOTS)),
            pltpu.SemaphoreType.DMA((8, 2, SLOTS)),
            pltpu.SemaphoreType.DMA((8,)),
            pltpu.SemaphoreType.DMA((8,)),
        ],
        compiler_params=pltpu.CompilerParams(
            collective_id=0, has_side_effects=True, vmem_limit_bytes=56 * 1024 * 1024
        ),
    )(electric, magnetic, material_ids, material_table)


def solution(mesh):
    placed = (P(None, "gx", "gy", None), P(None, "gx", "gy", None), P("gx", "gy", None), P())
    return jax.shard_map(
        shards,
        mesh=mesh,
        in_specs=placed,
        out_specs=(P(None, "gx", "gy", None), P(None, "gx", "gy", None)),
        check_vma=False,
    )
```

```python
import functools

import jax
import jax.numpy as jnp
import numpy as np
from jax import lax
from jax.experimental import pallas as pl
from jax.experimental.pallas import tpu as pltpu
from jax.sharding import PartitionSpec as P

STEPS = 12
MATS = 8
BLOCK = 6
MESH = pl.DeviceIdType.MESH
NX, NY, NZ = 16, 32, 128
PX = BLOCK + 1
PY = 16
XP, YP = NX + 2 * PX, NY + 2 * PY
DEEP = BLOCK
IDS = BLOCK - 1
SLOTS = 2 + 6 + 7
DIRS = ((-1, 0), (1, 0), (0, -1), (0, 1), (-1, 1), (1, 1), (-1, -1), (1, -1))
W, E, S, N, NW, NE, SW, SE = range(8)
OPPOSITE = (E, W, N, S, SE, SW, NE, NW)
TILES = (12, 12, 8, 8, 4, 4, 4, 4)
MID = (8, 8, 4, 4, 0, 0, 0, 0)


def after_z(a, lane):
    return jnp.where(lane < NZ - 1, pltpu.roll(a, NZ - 1, 2), 0.0)


def before_z(a, lane):
    return jnp.where(lane > 0, pltpu.roll(a, 1, 2), 0.0)


def update_h(e, h, x, planes, row, n):
    lane = lax.broadcasted_iota(jnp.int32, (planes, n, NZ), 2)
    xs, ahead, rows, up = pl.ds(x, planes), pl.ds(x + 1, planes), pl.ds(row, n), pl.ds(row + 1, n)
    e0, e1, e2 = (e[c, xs, rows] for c in range(3))
    c0 = (e[2, xs, up] - e2) - (after_z(e1, lane) - e1)
    c1 = (after_z(e0, lane) - e0) - (e[2, ahead, rows] - e2)
    c2 = (e[1, ahead, rows] - e1) - (e[0, xs, up] - e0)
    new = [h[c, xs, rows] - 0.45 * curl for c, curl in enumerate((c0, c1, c2))]
    for c in range(3):
        h[c, xs, rows] = new[c]


def update_e(e, h, k, j, amp, x, planes, row, n):
    lane = lax.broadcasted_iota(jnp.int32, (planes, n, NZ), 2)
    xs, behind, rows, down = pl.ds(x, planes), pl.ds(x - 1, planes), pl.ds(row, n), pl.ds(row - 1, n)
    krows = pl.ds(row - 8, n)
    h0, h1, h2 = (h[c, xs, rows] for c in range(3))
    c0 = (h2 - h[2, xs, down]) - (h1 - before_z(h1, lane))
    c1 = (h0 - before_z(h0, lane)) - (h2 - h[2, behind, rows])
    c2 = (h1 - h[1, behind, rows]) - (h0 - h[0, xs, down])
    xx, yy, zz, xy, xz, yz = (k[c, xs, krows] for c in range(6))
    new0 = e[0, xs, rows] + ((xx * c0 + xy * c1) + (xz * c2 - amp * j[0, xs, krows]))
    new1 = e[1, xs, rows] + ((xy * c0 + yy * c1) + (yz * c2 - amp * j[1, xs, krows]))
    new2 = e[2, xs, rows] + ((xz * c0 + yz * c1) + (zz * c2 - amp * j[2, xs, krows]))
    for c, new in enumerate((new0, new1, new2)):
        e[c, xs, rows] = new


def kernel(e_in, m_in, ids_in, table, e_out, m_out, et, ht, ef, hf, kk, jj, ids, own_x, own_y, ring, amps, *rest):
    out, inn = rest[:8], rest[8:16]
    out_sem, in_sem, id_out, id_in, local = rest[16:]
    gx, gy = lax.axis_index("gx"), lax.axis_index("gy")
    last_x, last_y = lax.axis_size("gx") - 1, lax.axis_size("gy") - 1

    def there(d):
        dx, dy = DIRS[d]
        checks = []
        if dx:
            checks.append(gx > 0 if dx < 0 else gx < last_x)
        if dy:
            checks.append(gy > 0 if dy < 0 else gy < last_y)
        return functools.reduce(jnp.logical_and, checks)

    def device(d):
        return (gx + DIRS[d][0], gy + DIRS[d][1])

    box = (pl.ds(PX, NX), pl.ds(PY, NY))

    def load(i):
        pairs = [(ids_in, ids.at[pl.ds(PX, NX), pl.ds(8, NY)])]
        for comp in range(3):
            pairs.append((e_in.at[comp], et.at[(comp, *box)]))
            pairs.append((m_in.at[comp], ht.at[(comp, *box)]))
        return pltpu.make_async_copy(*pairs[i], local.at[i])

    for i in range(7):
        load(i).start()
    def clear_pieces(slot, c):
        for d in range(8):
            mid, tiles = MID[d], TILES[d]
            inn[d][slot, pl.ds(mid, tiles - mid)] = jnp.zeros((tiles - mid, 8, NZ), jnp.float32)
        return c

    lax.fori_loop(0, SLOTS, clear_pieces, 0)
    barrier = pltpu.get_barrier_semaphore()
    for d in range(8):
        @pl.when(there(d))
        def _(d=d):
            pl.semaphore_signal(barrier, inc=1, device_id=device(d), device_id_type=MESH)
    def around(d):
        dx, dy = DIRS[d]
        xd = pl.ds(PX + NX if dx < 0 else PX - IDS, IDS) if dx else pl.ds(PX, NX)
        yd = pl.ds(8 + NY if dy < 0 else 8 - IDS, IDS) if dy else pl.ds(8, NY)
        return xd, yd

    def id_copy(d):
        xd, yd = around(d)
        dx, dy = DIRS[d]
        xs = pl.ds(0 if dx < 0 else NX - IDS, IDS) if dx else pl.ds(0, NX)
        ys = pl.ds(0 if dy < 0 else NY - IDS, IDS) if dy else pl.ds(0, NY)
        return pltpu.make_async_remote_copy(
            src_ref=ids_in.at[xs, ys],
            dst_ref=ids.at[xd, yd],
            send_sem=id_out.at[d],
            recv_sem=id_in.at[d],
            device_id=device(d),
            device_id_type=MESH,
        )

    for d in range(8):
        @pl.when(jnp.logical_not(there(OPPOSITE[d])))
        def _(d=d):
            xd, yd = around(d)
            ids[xd, yd] = jnp.full((xd.size, yd.size, NZ), -1, jnp.int32)

            if MID[d]:
                def clear(s, c):
                    inn[d][s, pl.ds(0, MID[d])] = jnp.zeros((MID[d], 8, NZ), jnp.float32)
                    return c

                lax.fori_loop(0, SLOTS, clear, 0)

    def clear_planes(x, c):
        for comp in range(3):
            jj[comp, x] = jnp.zeros((YP - 16, NZ), jnp.float32)
            for a in (ef, hf):
                a[comp, x] = jnp.zeros((YP, NZ), jnp.float32)
        return c

    lax.fori_loop(0, XP, clear_planes, 0)
    for step in range(STEPS):
        amps[step] = np.float32(np.sin(np.float32(0.3 * (step + 1))))

    def parts(d, depth, last):
        mid, pieces = MID[d], []
        before, after = pl.ds(DEEP - depth, depth), pl.ds(0, depth)
        if mid and not (depth == 0 and d in (E, N)) and not (last and d in (W, S)):
            pieces.append((pl.ds(0, mid), pl.ds(0, 8)))
        if depth:
            if mid:
                pieces.append((pl.ds(mid, 2 if last else 4), before if d in (W, S) else after))
            if d in (NW, SE):
                pieces.append((pl.ds(0, 2), before))
                if not last:
                    pieces.append((pl.ds(2, 2), after))
            if d == NE:
                pieces.append((pl.ds(0, 4), after))
            if d == SW and not last:
                pieces.append((pl.ds(0, 4), before))
        return pieces

    def each(do, slot, depth, last, sending):
        for d in range(8):
            pieces = parts(d, depth, last)
            if pieces:
                @pl.when(there(d if sending else OPPOSITE[d]))
                def _(d=d):
                    for which, (ts, rows) in enumerate(pieces):
                        do(pltpu.make_async_remote_copy(
                            src_ref=out[d].at[slot, ts, rows],
                            dst_ref=inn[d].at[slot, ts, rows],
                            send_sem=out_sem.at[d, which, slot],
                            recv_sem=in_sem.at[d, which, slot],
                            device_id=device(d),
                            device_id_type=MESH,
                        ))

    def each_of(depths, do, slot, depth, last, sending):
        for m in depths:
            @pl.when(depth == m)
            def _(m=m):
                each(do, slot, m, last, sending)

    def start(copy):
        copy.start()

    def arrive(copy):
        copy.wait_recv()

    def leave(copy):
        copy.wait_send()

    XA, XZ, YA, YZ = PX, PX + NX - 1, PY, PY + NY - 1

    def put_face(d, slot, at, a, comps, x):
        for i, c in enumerate(comps):
            out[d][slot, pl.ds(at + 4 * i, 4)] = a[c, x, pl.ds(YA, NY)].reshape(4, 8, NZ)

    def put_line(d, slot, at, a, comps, y):
        for i, c in enumerate(comps):
            out[d][slot, pl.ds(at + 2 * i, 2)] = a[c, pl.ds(XA, NX), y].reshape(2, 8, NZ)

    def put_piece_y(d, slot, at, a, x, top):
        for i, c in enumerate((1, 2)):
            out[d][slot, at + i] = a[c, x, pl.ds(YZ + 1 if top else YA - DEEP, 8)]

    def put_piece_x(d, slot, at, a, y, right):
        for i, c in enumerate((0, 2)):
            out[d][slot, at + i, pl.ds(0, DEEP)] = a[c, pl.ds(XZ + 1 if right else XA - DEEP, DEEP), y]

    def pack_e(slot, corners=True):
        put_face(W, slot, 0, ef, (1, 2), XA)
        put_line(S, slot, 0, ef, (0, 2), YA)
        for i, c in enumerate((1, 2)):
            own_x[slot, 2 + i] = ef[c, XZ + 1, pl.ds(YA, NY)]
        for i, c in enumerate((0, 2)):
            own_y[slot, 2 + i] = ef[c, pl.ds(XA, NX), YZ + 1]
        if corners:
            put_piece_x(W, slot, 10, ef, YZ + 1, False)
            put_piece_x(E, slot, 10, ef, YZ + 1, True)
            put_piece_y(S, slot, 6, ef, XZ + 1, False)
            put_piece_y(N, slot, 6, ef, XZ + 1, True)
            put_piece_y(NW, slot, 2, ef, XA, True)
            put_piece_y(SW, slot, 0, ef, XA, False)
            put_piece_x(SW, slot, 2, ef, YA, False)
            put_piece_x(SE, slot, 2, ef, YA, True)

    def pack_h(slot):
        put_face(E, slot, 0, hf, (1, 2), XZ)
        put_line(N, slot, 0, hf, (0, 2), YZ)
        for i, c in enumerate((1, 2)):
            own_x[slot, i] = hf[c, XA - 1, pl.ds(YA, NY)]
        for i, c in enumerate((0, 2)):
            own_y[slot, i] = hf[c, pl.ds(XA, NX), YA - 1]
        put_piece_x(W, slot, 8, hf, YA - 1, False)
        put_piece_x(E, slot, 8, hf, YA - 1, True)
        put_piece_y(S, slot, 4, hf, XA - 1, False)
        put_piece_y(N, slot, 4, hf, XA - 1, True)
        put_piece_x(NW, slot, 0, hf, YZ, False)
        put_piece_y(NE, slot, 0, hf, XZ, True)
        put_piece_x(NE, slot, 2, hf, YZ, True)
        put_piece_y(SE, slot, 0, hf, XZ, False)

    def ring_x(a, x, slot, own, face, low, high):
        for i, c in enumerate((1, 2)):
            d, at = face
            a[c, x, pl.ds(YA, NY)] = own_x[slot, own + i] + inn[d][slot, pl.ds(at + 4 * i, 4)].reshape(NY, NZ)
            for pieces, row in ((low, YA), (high, YA + NY - DEEP)):
                (d1, at1), (d2, at2) = pieces
                some = pl.ds(0, DEEP)
                a[c, x, pl.ds(row, DEEP)] += inn[d1][slot, at1 + i, some] + inn[d2][slot, at2 + i, some]

    def ring_y(a, y, slot, own, face, low, high):
        for i, c in enumerate((0, 2)):
            d, at = face
            ring[...] = own_y[slot, own + i] + inn[d][slot, pl.ds(at + 2 * i, 2)].reshape(NX, NZ)
            for pieces, row in ((low, 0), (high, NX - DEEP)):
                (d1, at1), (d2, at2) = pieces
                some = pl.ds(0, DEEP)
                ring[pl.ds(row, DEEP)] += inn[d1][slot, at1 + i, some] + inn[d2][slot, at2 + i, some]
            a[c, pl.ds(XA, NX), y] = ring[...]

    def ring_e(slot):
        ring_x(et, XZ + 1, slot, 2, (W, 0), ((N, 6), (NW, 2)), ((S, 6), (SW, 0)))
        ring_y(et, YZ + 1, slot, 2, (S, 0), ((E, 10), (SE, 2)), ((W, 10), (SW, 2)))

    def ring_h(slot):
        ring_x(ht, XA - 1, slot, 0, (E, 0), ((N, 4), (NE, 0)), ((S, 4), (SE, 0)))
        ring_y(ht, YA - 1, slot, 0, (N, 0), ((E, 8), (NE, 2)), ((W, 8), (NW, 0)))

    def look(x, planes, row, n, source):
        xs, rows = pl.ds(x, planes), pl.ds(row, n)
        here = ids[xs, rows]
        bits = [(here & (1 << b)) != 0 for b in range(3)]
        real = here >= 0

        def pick(c):
            level = [table[m, c] for m in range(MATS)]
            for b in range(3):
                level = [jnp.where(bits[b], level[2 * i + 1], level[2 * i]) for i in range(len(level) // 2)]
            return level[0]

        tensor = [jnp.where(real, 0.45 * pick(c), 0.0) for c in range(6)]
        for c in range(6):
            kk[c, xs, rows] = tensor[c]
        if source:
            xx, yy, zz, xy, xz, yz = tensor
            s0, s1, s2 = (pick(c) for c in (6, 7, 8))
            jj[0, xs, rows] = xx * s0 + xy * s1 + xz * s2
            jj[1, xs, rows] = xy * s0 + yy * s1 + yz * s2
            jj[2, xs, rows] = xz * s0 + yz * s1 + zz * s2

    def look_own(i, c):
        look(PX + 2 * i, 2, 8, NY, True)
        return c

    def look_rows(i, c):
        look(PX + 4 * i, 4, 0, 8, False)
        look(PX + 4 * i, 4, 8 + NY, 8, False)
        return c

    def look_planes(i, c):
        look(PX - IDS + i, 1, 0, NY + 16, False)
        look(PX + NX + i, 1, 0, NY + 16, False)
        return c

    def frame(update):
        wide, halo = BLOCK - 1, BLOCK // 2
        update(PX - wide, NX + 2 * wide, 8, 16)
        update(PX - wide, NX + 2 * wide, 40, 16)
        update(PX - halo - 1, halo + BLOCK, 24, 16)
        update(PX + NX - BLOCK, halo + BLOCK, 24, 16)

    def lines_h(update):
        update(PX - BLOCK, NX + 2 * BLOCK, 8, 8)
        update(PX - BLOCK, NX + 2 * BLOCK, 40, 8)
        for x in (PX - 1, PX + NX - 1):
            update(x, 1, 16, 24)
            update(x, 1, 48, 8)

    def copy_in(i, c):
        xs = pl.ds(PX + 2 * i, 2)
        for comp in range(3):
            for a, t in ((ef, et), (hf, ht)):
                a[comp, xs, pl.ds(8, 8)] = jnp.zeros((2, 8, NZ), jnp.float32)
                a[comp, xs, pl.ds(PY, NY)] = t[comp, xs, pl.ds(PY, NY)]
                a[comp, xs, pl.ds(PY + NY, 8)] = jnp.zeros((2, 8, NZ), jnp.float32)
        return c

    def zero_plane(x, c):
        for comp in range(3):
            for a in (ef, hf):
                a[comp, x, pl.ds(8, NY + 16)] = jnp.zeros((NY + 16, NZ), jnp.float32)
        return c

    def edges_h():
        @pl.when(gx == 0)
        def _():
            for comp in range(3):
                hf[comp, PX - 1, pl.ds(8, NY + 16)] = jnp.zeros((NY + 16, NZ), jnp.float32)

        @pl.when(gy == 0)
        def _():
            for comp in range(3):
                hf[comp, :, pl.ds(8, 8)] = jnp.zeros((XP, 8, NZ), jnp.float32)

    def true_step(step, slot):
        ring_e(slot - 1)
        ring_h(slot)
        update_h(et, ht, PX, NX, PY, NY)
        update_e(et, ht, kk, jj, amps[step], PX, NX, PY, NY)

    load(0).wait()
    lax.fori_loop(0, NX // 2, look_own, 0)
    for i in range(1, 7):
        load(i).wait()
    lax.fori_loop(0, NX // 2, copy_in, 0)
    pack_e(0, corners=False)
    lines_h(functools.partial(update_h, ef, hf))
    edges_h()
    pack_h(1)
    peers = sum(there(d).astype(jnp.int32) for d in range(8))
    pl.semaphore_wait(barrier, peers)
    each(start, 0, 0, False, True)
    each(start, 1, 1, True, True)
    for d in range(8):
        @pl.when(there(d))
        def _(d=d):
            id_copy(d).start()
    each(arrive, 0, 0, False, False)
    each(arrive, 1, 1, True, False)
    true_step(0, 1)
    for d in range(8):
        @pl.when(there(OPPOSITE[d]))
        def _(d=d):
            id_copy(d).wait_recv()
    lax.fori_loop(0, NX // 4, look_rows, 0)
    lax.fori_loop(0, IDS, look_planes, 0)

    def block(b, c):
        size, begin, base = 4 + b, 5 * b - 4, 6 * b - 4
        lax.fori_loop(0, NX // 2, copy_in, 0)
        lax.fori_loop(0, PX, zero_plane, 0)
        lax.fori_loop(PX + NX, XP, zero_plane, 0)
        pack_e(base, corners=False)
        each(start, base, 0, False, True)

        def free(t, c):
            frame(functools.partial(update_h, ef, hf))
            edges_h()
            frame(functools.partial(update_e, ef, hf, kk, jj, amps[begin + t - 1]))
            pack_e(base + t)
            pack_h(base + t)
            each_of(range(1, BLOCK), start, base + t, t, False, True)
            return c

        lax.fori_loop(1, size, free, 0)
        lines_h(functools.partial(update_h, ef, hf))
        edges_h()
        pack_h(base + size)
        each_of((BLOCK - 1, BLOCK), start, base + size, size, True, True)
        each(arrive, base, 0, False, False)

        def true(t, c):
            @pl.when(t < size)
            def _():
                each_of(range(1, BLOCK), arrive, base + t, t, False, False)

            @pl.when(t == size)
            def _():
                each_of((BLOCK - 1, BLOCK), arrive, base + t, t, True, False)

            true_step(begin + t - 1, base + t)
            return c

        lax.fori_loop(1, size + 1, true, 0)
        return c

    lax.fori_loop(1, 3, block, 0)

    def stores():
        pairs = [(a.at[(comp, *box)], o.at[comp]) for a, o in ((et, e_out), (ht, m_out)) for comp in range(3)]
        return [pltpu.make_async_copy(src, dst, local.at[1 + i]) for i, (src, dst) in enumerate(pairs)]

    for copy in stores():
        copy.start()

    for d in range(8):
        @pl.when(there(d))
        def _(d=d):
            id_copy(d).wait_send()

    each(leave, 0, 0, False, True)
    each(leave, 1, 1, True, True)

    def drain(b, c):
        size, base = 4 + b, 6 * b - 4
        each(leave, base, 0, False, True)

        def one(t, c):
            each_of(range(1, BLOCK), leave, base + t, t, False, True)
            return c

        lax.fori_loop(1, size, one, 0)
        each_of((BLOCK - 1, BLOCK), leave, base + size, size, True, True)
        return c

    lax.fori_loop(1, 3, drain, 0)
    for copy in stores():
        copy.wait()


def shards(electric, magnetic, material_ids, material_table):
    field = jax.ShapeDtypeStruct((3, NX, NY, NZ), jnp.float32)
    hbm = pl.BlockSpec(memory_space=pl.ANY)
    big = pltpu.VMEM((3, XP, YP, NZ), jnp.float32)
    messages = [pltpu.VMEM((SLOTS, TILES[d], 8, NZ), jnp.float32) for d in range(8)]
    return pl.pallas_call(
        kernel,
        out_shape=(field, field),
        in_specs=[hbm, hbm, hbm, pl.BlockSpec(memory_space=pltpu.SMEM)],
        out_specs=(hbm, hbm),
        scratch_shapes=[
            big,
            big,
            big,
            big,
            pltpu.VMEM((6, XP, YP - 16, NZ), jnp.float32),
            pltpu.VMEM((3, XP, YP - 16, NZ), jnp.float32),
            pltpu.VMEM((XP, YP - 16, NZ), jnp.int32),
            pltpu.VMEM((SLOTS, 4, NY, NZ), jnp.float32),
            pltpu.VMEM((SLOTS, 4, NX, NZ), jnp.float32),
            pltpu.VMEM((NX, NZ), jnp.float32),
            pltpu.SMEM((STEPS,), jnp.float32),
            *messages,
            *messages,
            pltpu.SemaphoreType.DMA((8, 2, SLOTS)),
            pltpu.SemaphoreType.DMA((8, 2, SLOTS)),
            pltpu.SemaphoreType.DMA((8,)),
            pltpu.SemaphoreType.DMA((8,)),
            pltpu.SemaphoreType.DMA((7,)),
        ],
        compiler_params=pltpu.CompilerParams(
            collective_id=0, has_side_effects=True, vmem_limit_bytes=56 * 1024 * 1024
        ),
    )(electric, magnetic, material_ids, material_table)


def solution(mesh):
    placed = (P(None, "gx", "gy", None), P(None, "gx", "gy", None), P("gx", "gy", None), P())
    return jax.shard_map(
        shards,
        mesh=mesh,
        in_specs=placed,
        out_specs=(P(None, "gx", "gy", None), P(None, "gx", "gy", None)),
        check_vma=False,
    )
```

```python
import functools

import jax
import jax.numpy as jnp
import numpy as np
from jax import lax
from jax.experimental import pallas as pl
from jax.experimental.pallas import tpu as pltpu
from jax.sharding import PartitionSpec as P

STEPS = 12
MATS = 8
BLOCK = 6
MESH = pl.DeviceIdType.MESH
NX, NY, NZ = 16, 32, 128
PX = BLOCK + 1
PY = 16
XP, YP = NX + 2 * PX, NY + 2 * PY
DEEP = BLOCK
IDS = BLOCK - 1
SIZES = (1, 5, 6)
SLOTS = 2 + 6 + 7
DIRS = ((-1, 0), (1, 0), (0, -1), (0, 1), (-1, 1), (1, 1), (-1, -1), (1, -1))
W, E, S, N, NW, NE, SW, SE = range(8)
OPPOSITE = (E, W, N, S, SE, SW, NE, NW)
TILES = (12, 12, 8, 8, 4, 4, 4, 4)
MID = (8, 8, 4, 4, 0, 0, 0, 0)


def after_z(a, lane):
    return jnp.where(lane < NZ - 1, pltpu.roll(a, NZ - 1, 2), 0.0)


def before_z(a, lane):
    return jnp.where(lane > 0, pltpu.roll(a, 1, 2), 0.0)


def update_h(e, h, x, planes, row, n):
    lane = lax.broadcasted_iota(jnp.int32, (planes, n, NZ), 2)
    xs, ahead, rows, up = pl.ds(x, planes), pl.ds(x + 1, planes), pl.ds(row, n), pl.ds(row + 1, n)
    e0, e1, e2 = (e[c, xs, rows] for c in range(3))
    c0 = (e[2, xs, up] - e2) - (after_z(e1, lane) - e1)
    c1 = (after_z(e0, lane) - e0) - (e[2, ahead, rows] - e2)
    c2 = (e[1, ahead, rows] - e1) - (e[0, xs, up] - e0)
    new = [h[c, xs, rows] - 0.45 * curl for c, curl in enumerate((c0, c1, c2))]
    for c in range(3):
        h[c, xs, rows] = new[c]


def update_e(e, h, k, j, amp, x, planes, row, n):
    lane = lax.broadcasted_iota(jnp.int32, (planes, n, NZ), 2)
    xs, behind, rows, down = pl.ds(x, planes), pl.ds(x - 1, planes), pl.ds(row, n), pl.ds(row - 1, n)
    krows = pl.ds(row - 8, n)
    h0, h1, h2 = (h[c, xs, rows] for c in range(3))
    c0 = (h2 - h[2, xs, down]) - (h1 - before_z(h1, lane))
    c1 = (h0 - before_z(h0, lane)) - (h2 - h[2, behind, rows])
    c2 = (h1 - h[1, behind, rows]) - (h0 - h[0, xs, down])
    xx, yy, zz, xy, xz, yz = (k[c, xs, krows] for c in range(6))
    new0 = e[0, xs, rows] + ((xx * c0 + xy * c1) + (xz * c2 - amp * j[0, xs, krows]))
    new1 = e[1, xs, rows] + ((xy * c0 + yy * c1) + (yz * c2 - amp * j[1, xs, krows]))
    new2 = e[2, xs, rows] + ((xz * c0 + yz * c1) + (zz * c2 - amp * j[2, xs, krows]))
    for c, new in enumerate((new0, new1, new2)):
        e[c, xs, rows] = new


def kernel(e_in, m_in, ids_in, table, e_out, m_out, et, ht, ef, hf, kk, jj, ids, own_x, own_y, ring, total, amps, *rest):
    out, inn = rest[:8], rest[8:16]
    out_sem, in_sem, id_out, id_in, local = rest[16:]
    gx, gy = lax.axis_index("gx"), lax.axis_index("gy")
    last_x, last_y = lax.axis_size("gx") - 1, lax.axis_size("gy") - 1

    def there(d):
        dx, dy = DIRS[d]
        checks = []
        if dx:
            checks.append(gx > 0 if dx < 0 else gx < last_x)
        if dy:
            checks.append(gy > 0 if dy < 0 else gy < last_y)
        return functools.reduce(jnp.logical_and, checks)

    def device(d):
        return (gx + DIRS[d][0], gy + DIRS[d][1])

    box = (pl.ds(PX, NX), pl.ds(PY, NY))

    def load(i):
        pairs = [(ids_in, ids.at[pl.ds(PX, NX), pl.ds(8, NY)])]
        for comp in range(3):
            pairs.append((e_in.at[comp], et.at[(comp, *box)]))
            pairs.append((m_in.at[comp], ht.at[(comp, *box)]))
        return pltpu.make_async_copy(*pairs[i], local.at[i])

    for i in range(7):
        load(i).start()
    def clear_pieces(slot, c):
        for d in range(8):
            mid, tiles = MID[d], TILES[d]
            inn[d][slot, pl.ds(mid, tiles - mid)] = jnp.zeros((tiles - mid, 8, NZ), jnp.float32)
        return c

    lax.fori_loop(0, SLOTS, clear_pieces, 0)
    barrier = pltpu.get_barrier_semaphore()
    for d in range(8):
        @pl.when(there(d))
        def _(d=d):
            pl.semaphore_signal(barrier, inc=1, device_id=device(d), device_id_type=MESH)
    def around(d):
        dx, dy = DIRS[d]
        xd = pl.ds(PX + NX if dx < 0 else PX - IDS, IDS) if dx else pl.ds(PX, NX)
        yd = pl.ds(8 + NY if dy < 0 else 8 - IDS, IDS) if dy else pl.ds(8, NY)
        return xd, yd

    def id_copy(d):
        xd, yd = around(d)
        dx, dy = DIRS[d]
        xs = pl.ds(0 if dx < 0 else NX - IDS, IDS) if dx else pl.ds(0, NX)
        ys = pl.ds(0 if dy < 0 else NY - IDS, IDS) if dy else pl.ds(0, NY)
        return pltpu.make_async_remote_copy(
            src_ref=ids_in.at[xs, ys],
            dst_ref=ids.at[xd, yd],
            send_sem=id_out.at[d],
            recv_sem=id_in.at[d],
            device_id=device(d),
            device_id_type=MESH,
        )

    for d in range(8):
        @pl.when(jnp.logical_not(there(OPPOSITE[d])))
        def _(d=d):
            xd, yd = around(d)
            ids[xd, yd] = jnp.full((xd.size, yd.size, NZ), -1, jnp.int32)

            if MID[d]:
                def clear(s, c):
                    inn[d][s, pl.ds(0, MID[d])] = jnp.zeros((MID[d], 8, NZ), jnp.float32)
                    return c

                lax.fori_loop(0, SLOTS, clear, 0)

    def clear_planes(x, c):
        for comp in range(3):
            jj[comp, x] = jnp.zeros((YP - 16, NZ), jnp.float32)
            for a in (ef, hf):
                a[comp, x] = jnp.zeros((YP, NZ), jnp.float32)
        return c

    lax.fori_loop(0, XP, clear_planes, 0)
    for step in range(STEPS):
        amps[step] = np.float32(np.sin(np.float32(0.3 * (step + 1))))

    def parts(d, depth, last):
        mid, pieces = MID[d], []
        before, after, less = pl.ds(DEEP - depth, depth), pl.ds(0, depth), pl.ds(0, depth - 1)
        if mid and not (depth == 0 and d in (E, N)) and not (last and d in (W, S)):
            pieces.append((pl.ds(0, mid), pl.ds(0, 8)))
        if depth:
            if mid:
                if d in (W, S):
                    pieces.append((pl.ds(mid, 2 if last else 4), before))
                else:
                    if depth > 1:
                        pieces.append((pl.ds(mid, 2), less))
                    if not last:
                        pieces.append((pl.ds(mid + 2, 2), after))
            if d in (NW, SE):
                pieces.append((pl.ds(0, 2), before))
                if not last:
                    pieces.append((pl.ds(2, 2), after))
            if d == NE and depth > 1:
                pieces.append((pl.ds(0, 4), less))
            if d == SW and not last:
                pieces.append((pl.ds(0, 4), before))
        return pieces

    def rows_of(d, depth, last):
        return sum(ts.size * rows.size for ts, rows in parts(d, depth, last))

    def start(slot, depth, last):
        for d in range(8):
            if parts(d, depth, last):
                @pl.when(there(d))
                def _(d=d):
                    for ts, rows in parts(d, depth, last):
                        pltpu.make_async_remote_copy(
                            src_ref=out[d].at[slot, ts, rows],
                            dst_ref=inn[d].at[slot, ts, rows],
                            send_sem=out_sem.at[d],
                            recv_sem=in_sem.at[d, slot],
                            device_id=device(d),
                            device_id_type=MESH,
                        ).start()

    def all_of(rows, sem):
        some = total.at[pl.ds(0, rows)]
        return pltpu.make_async_copy(some, some, sem)

    def arrive(slot, depth, last):
        for d in range(8):
            if parts(d, depth, last):
                @pl.when(there(OPPOSITE[d]))
                def _(d=d):
                    all_of(rows_of(d, depth, last), in_sem.at[d, slot]).wait()

    def leave():
        for d in range(8):
            @pl.when(there(d))
            def _(d=d):
                rows = 0
                for size in SIZES:
                    rows += sum(rows_of(d, m, m == size) for m in range(size + 1))
                all_of(rows, out_sem.at[d]).wait()

    def one_of(depths, do, slot, depth, last):
        for m in depths:
            @pl.when(depth == m)
            def _(m=m):
                do(slot, m, last)

    XA, XZ, YA, YZ = PX, PX + NX - 1, PY, PY + NY - 1

    def put_face(d, slot, at, a, comps, x):
        for i, c in enumerate(comps):
            out[d][slot, pl.ds(at + 4 * i, 4)] = a[c, x, pl.ds(YA, NY)].reshape(4, 8, NZ)

    def put_line(d, slot, at, a, comps, y):
        for i, c in enumerate(comps):
            out[d][slot, pl.ds(at + 2 * i, 2)] = a[c, pl.ds(XA, NX), y].reshape(2, 8, NZ)

    def put_piece_y(d, slot, at, a, x, top):
        for i, c in enumerate((1, 2)):
            out[d][slot, at + i] = a[c, x, pl.ds(YZ + 1 if top else YA - DEEP, 8)]

    def put_piece_x(d, slot, at, a, y, right):
        for i, c in enumerate((0, 2)):
            out[d][slot, at + i, pl.ds(0, DEEP)] = a[c, pl.ds(XZ + 1 if right else XA - DEEP, DEEP), y]

    def pack_first(slot):
        put_face(W, slot, 0, et, (1, 2), XA)
        put_line(S, slot, 0, et, (0, 2), YA)
        own_x[slot, pl.ds(2, 2)] = jnp.zeros((2, NY, NZ), jnp.float32)
        own_y[slot, pl.ds(2, 2)] = jnp.zeros((2, NX, NZ), jnp.float32)

    def pack_e(slot):
        put_face(W, slot, 0, ef, (1, 2), XA)
        put_line(S, slot, 0, ef, (0, 2), YA)
        for i, c in enumerate((1, 2)):
            own_x[slot, 2 + i] = ef[c, XZ + 1, pl.ds(YA, NY)]
        for i, c in enumerate((0, 2)):
            own_y[slot, 2 + i] = ef[c, pl.ds(XA, NX), YZ + 1]
        put_piece_x(W, slot, 10, ef, YZ + 1, False)
        put_piece_x(E, slot, 10, ef, YZ + 1, True)
        put_piece_y(S, slot, 6, ef, XZ + 1, False)
        put_piece_y(N, slot, 6, ef, XZ + 1, True)
        put_piece_y(NW, slot, 2, ef, XA, True)
        put_piece_y(SW, slot, 0, ef, XA, False)
        put_piece_x(SW, slot, 2, ef, YA, False)
        put_piece_x(SE, slot, 2, ef, YA, True)

    def pack_h(slot):
        put_face(E, slot, 0, hf, (1, 2), XZ)
        put_line(N, slot, 0, hf, (0, 2), YZ)
        for i, c in enumerate((1, 2)):
            own_x[slot, i] = hf[c, XA - 1, pl.ds(YA, NY)]
        for i, c in enumerate((0, 2)):
            own_y[slot, i] = hf[c, pl.ds(XA, NX), YA - 1]
        put_piece_x(W, slot, 8, hf, YA - 1, False)
        put_piece_x(E, slot, 8, hf, YA - 1, True)
        put_piece_y(S, slot, 4, hf, XA - 1, False)
        put_piece_y(N, slot, 4, hf, XA - 1, True)
        put_piece_x(NW, slot, 0, hf, YZ, False)
        put_piece_y(NE, slot, 0, hf, XZ, True)
        put_piece_x(NE, slot, 2, hf, YZ, True)
        put_piece_y(SE, slot, 0, hf, XZ, False)

    def ring_x(a, x, slot, own, face, low, high):
        for i, c in enumerate((1, 2)):
            d, at = face
            a[c, x, pl.ds(YA, NY)] = own_x[slot, own + i] + inn[d][slot, pl.ds(at + 4 * i, 4)].reshape(NY, NZ)
            for pieces, row in ((low, YA), (high, YA + NY - DEEP)):
                (d1, at1), (d2, at2) = pieces
                some = pl.ds(0, DEEP)
                a[c, x, pl.ds(row, DEEP)] += inn[d1][slot, at1 + i, some] + inn[d2][slot, at2 + i, some]

    def ring_y(a, y, slot, own, face, low, high):
        for i, c in enumerate((0, 2)):
            d, at = face
            ring[...] = own_y[slot, own + i] + inn[d][slot, pl.ds(at + 2 * i, 2)].reshape(NX, NZ)
            for pieces, row in ((low, 0), (high, NX - DEEP)):
                (d1, at1), (d2, at2) = pieces
                some = pl.ds(0, DEEP)
                ring[pl.ds(row, DEEP)] += inn[d1][slot, at1 + i, some] + inn[d2][slot, at2 + i, some]
            a[c, pl.ds(XA, NX), y] = ring[...]

    def ring_e(slot):
        ring_x(et, XZ + 1, slot, 2, (W, 0), ((N, 6), (NW, 2)), ((S, 6), (SW, 0)))
        ring_y(et, YZ + 1, slot, 2, (S, 0), ((E, 10), (SE, 2)), ((W, 10), (SW, 2)))

    def ring_h(slot):
        ring_x(ht, XA - 1, slot, 0, (E, 0), ((N, 4), (NE, 0)), ((S, 4), (SE, 0)))
        ring_y(ht, YA - 1, slot, 0, (N, 0), ((E, 8), (NE, 2)), ((W, 8), (NW, 0)))

    def look(x, planes, row, n, source):
        xs, rows = pl.ds(x, planes), pl.ds(row, n)
        here = ids[xs, rows]
        bits = [(here & (1 << b)) != 0 for b in range(3)]
        real = here >= 0

        def pick(c):
            level = [table[m, c] for m in range(MATS)]
            for b in range(3):
                level = [jnp.where(bits[b], level[2 * i + 1], level[2 * i]) for i in range(len(level) // 2)]
            return level[0]

        tensor = [jnp.where(real, 0.45 * pick(c), 0.0) for c in range(6)]
        for c in range(6):
            kk[c, xs, rows] = tensor[c]
        if source:
            xx, yy, zz, xy, xz, yz = tensor
            s0, s1, s2 = (pick(c) for c in (6, 7, 8))
            jj[0, xs, rows] = xx * s0 + xy * s1 + xz * s2
            jj[1, xs, rows] = xy * s0 + yy * s1 + yz * s2
            jj[2, xs, rows] = xz * s0 + yz * s1 + zz * s2

    def look_own(i, c):
        look(PX + 2 * i, 2, 8, NY, True)
        return c

    def look_rows(i, c):
        look(PX + 4 * i, 4, 0, 8, False)
        look(PX + 4 * i, 4, 8 + NY, 8, False)
        return c

    def look_planes(i, c):
        look(PX - IDS + i, 1, 0, NY + 16, False)
        look(PX + NX + i, 1, 0, NY + 16, False)
        return c

    def frame(update):
        wide, halo = BLOCK - 1, BLOCK // 2
        update(PX - wide, NX + 2 * wide, 8, 16)
        update(PX - wide, NX + 2 * wide, 40, 16)
        update(PX - halo - 1, halo + BLOCK, 24, 16)
        update(PX + NX - BLOCK, halo + BLOCK, 24, 16)

    def lines_h(update):
        update(PX - BLOCK, NX + 2 * BLOCK, 8, 8)
        update(PX - BLOCK, NX + 2 * BLOCK, 40, 8)
        for x in (PX - 1, PX + NX - 1):
            update(x, 1, 16, 24)
            update(x, 1, 48, 8)

    def copy_in(i, c):
        xs = pl.ds(PX + 2 * i, 2)
        for comp in range(3):
            for a, t in ((ef, et), (hf, ht)):
                a[comp, xs, pl.ds(8, 8)] = jnp.zeros((2, 8, NZ), jnp.float32)
                a[comp, xs, pl.ds(PY, NY)] = t[comp, xs, pl.ds(PY, NY)]
                a[comp, xs, pl.ds(PY + NY, 8)] = jnp.zeros((2, 8, NZ), jnp.float32)
        return c

    def zero_plane(x, c):
        for comp in range(3):
            for a in (ef, hf):
                a[comp, x, pl.ds(8, NY + 16)] = jnp.zeros((NY + 16, NZ), jnp.float32)
                a[comp, x + PX + NX, pl.ds(8, NY + 16)] = jnp.zeros((NY + 16, NZ), jnp.float32)
        return c

    def edges_h():
        @pl.when(gx == 0)
        def _():
            for comp in range(3):
                hf[comp, PX - 1, pl.ds(8, NY + 16)] = jnp.zeros((NY + 16, NZ), jnp.float32)

        @pl.when(gy == 0)
        def _():
            for comp in range(3):
                hf[comp, :, pl.ds(8, 8)] = jnp.zeros((XP, 8, NZ), jnp.float32)

    def true_step(step, slot):
        ring_e(slot - 1)
        ring_h(slot)
        update_h(et, ht, PX, NX, PY, NY)
        update_e(et, ht, kk, jj, amps[step], PX, NX, PY, NY)

    load(0).wait()
    lax.fori_loop(0, NX // 2, look_own, 0)
    for i in range(1, 7):
        load(i).wait()
    lax.fori_loop(0, NX // 2, copy_in, 0)
    pack_first(0)
    lines_h(functools.partial(update_h, ef, hf))
    edges_h()
    pack_h(1)
    peers = sum(there(d).astype(jnp.int32) for d in range(8))
    pl.semaphore_wait(barrier, peers)
    start(0, 0, False)
    start(1, 1, True)
    for d in range(8):
        @pl.when(there(d))
        def _(d=d):
            id_copy(d).start()
    arrive(0, 0, False)
    arrive(1, 1, True)
    true_step(0, 1)
    def look_around():
        for d in range(8):
            @pl.when(there(OPPOSITE[d]))
            def _(d=d):
                id_copy(d).wait_recv()
        lax.fori_loop(0, NX // 4, look_rows, 0)
        lax.fori_loop(0, IDS, look_planes, 0)

    def block(b, c):
        size, begin, base = 4 + b, 5 * b - 4, 6 * b - 4
        pack_first(base)
        start(base, 0, False)
        lax.fori_loop(0, NX // 2, copy_in, 0)
        lax.fori_loop(0, PX, zero_plane, 0)

        def free(t, c):
            frame(functools.partial(update_h, ef, hf))
            edges_h()

            @pl.when((b == 1) & (t == 1))
            def _():
                look_around()

            frame(functools.partial(update_e, ef, hf, kk, jj, amps[begin + t - 1]))
            pack_e(base + t)
            pack_h(base + t)
            one_of(range(1, BLOCK), start, base + t, t, False)
            return c

        lax.fori_loop(1, size, free, 0)
        lines_h(functools.partial(update_h, ef, hf))
        edges_h()
        pack_h(base + size)
        one_of((BLOCK - 1, BLOCK), start, base + size, size, True)
        arrive(base, 0, False)

        def true(t, c):
            @pl.when(t < size)
            def _():
                one_of(range(1, BLOCK), arrive, base + t, t, False)

            @pl.when(t == size)
            def _():
                one_of((BLOCK - 1, BLOCK), arrive, base + t, t, True)

            true_step(begin + t - 1, base + t)
            return c

        lax.fori_loop(1, size + 1, true, 0)
        return c

    lax.fori_loop(1, 3, block, 0)

    def stores():
        pairs = [(a.at[(comp, *box)], o.at[comp]) for a, o in ((et, e_out), (ht, m_out)) for comp in range(3)]
        return [pltpu.make_async_copy(src, dst, local.at[1 + i]) for i, (src, dst) in enumerate(pairs)]

    for copy in stores():
        copy.start()

    for d in range(8):
        @pl.when(there(d))
        def _(d=d):
            id_copy(d).wait_send()

    leave()
    for copy in stores():
        copy.wait()


def shards(electric, magnetic, material_ids, material_table):
    field = jax.ShapeDtypeStruct((3, NX, NY, NZ), jnp.float32)
    hbm = pl.BlockSpec(memory_space=pl.ANY)
    big = pltpu.VMEM((3, XP, YP, NZ), jnp.float32)
    messages = [pltpu.VMEM((SLOTS, TILES[d], 8, NZ), jnp.float32) for d in range(8)]
    return pl.pallas_call(
        kernel,
        out_shape=(field, field),
        in_specs=[hbm, hbm, hbm, pl.BlockSpec(memory_space=pltpu.SMEM)],
        out_specs=(hbm, hbm),
        scratch_shapes=[
            big,
            big,
            big,
            big,
            pltpu.VMEM((6, XP, YP - 16, NZ), jnp.float32),
            pltpu.VMEM((3, XP, YP - 16, NZ), jnp.float32),
            pltpu.VMEM((XP, YP - 16, NZ), jnp.int32),
            pltpu.VMEM((SLOTS, 4, NY, NZ), jnp.float32),
            pltpu.VMEM((SLOTS, 4, NX, NZ), jnp.float32),
            pltpu.VMEM((NX, NZ), jnp.float32),
            pltpu.VMEM((2048, NZ), jnp.float32),
            pltpu.SMEM((STEPS,), jnp.float32),
            *messages,
            *messages,
            pltpu.SemaphoreType.DMA((8,)),
            pltpu.SemaphoreType.DMA((8, SLOTS)),
            pltpu.SemaphoreType.DMA((8,)),
            pltpu.SemaphoreType.DMA((8,)),
            pltpu.SemaphoreType.DMA((7,)),
        ],
        compiler_params=pltpu.CompilerParams(
            collective_id=0, has_side_effects=True, vmem_limit_bytes=56 * 1024 * 1024
        ),
    )(electric, magnetic, material_ids, material_table)


def solution(mesh):
    placed = (P(None, "gx", "gy", None), P(None, "gx", "gy", None), P("gx", "gy", None), P())
    return jax.shard_map(
        shards,
        mesh=mesh,
        in_specs=placed,
        out_specs=(P(None, "gx", "gy", None), P(None, "gx", "gy", None)),
        check_vma=False,
    )
```

```python
import functools

import jax
import jax.numpy as jnp
import numpy as np
from jax import lax
from jax.experimental import pallas as pl
from jax.experimental.pallas import tpu as pltpu
from jax.sharding import PartitionSpec as P

STEPS = 12
MATS = 8
BLOCK = 6
MESH = pl.DeviceIdType.MESH
NX, NY, NZ = 16, 32, 128
PX = BLOCK + 1
PY = 16
XP, YP = NX + 2 * PX, NY + 2 * PY
DEEP = BLOCK
IDS = BLOCK - 1
SIZES = (1, 5, 6)
SLOTS = 2 + 6 + 7
DIRS = ((-1, 0), (1, 0), (0, -1), (0, 1), (-1, 1), (1, 1), (-1, -1), (1, -1))
W, E, S, N, NW, NE, SW, SE = range(8)
OPPOSITE = (E, W, N, S, SE, SW, NE, NW)
TILES = (12, 12, 8, 8, 4, 4, 4, 4)
MID = (8, 8, 4, 4, 0, 0, 0, 0)


def after_z(a, lane):
    return jnp.where(lane < NZ - 1, pltpu.roll(a, NZ - 1, 2), 0.0)


def before_z(a, lane):
    return jnp.where(lane > 0, pltpu.roll(a, 1, 2), 0.0)


def update_h(e, h, x, planes, row, n):
    lane = lax.broadcasted_iota(jnp.int32, (planes, n, NZ), 2)
    xs, ahead, rows, up = pl.ds(x, planes), pl.ds(x + 1, planes), pl.ds(row, n), pl.ds(row + 1, n)
    e0, e1, e2 = (e[c, xs, rows] for c in range(3))
    c0 = (e[2, xs, up] - e2) - (after_z(e1, lane) - e1)
    c1 = (after_z(e0, lane) - e0) - (e[2, ahead, rows] - e2)
    c2 = (e[1, ahead, rows] - e1) - (e[0, xs, up] - e0)
    new = [h[c, xs, rows] - 0.45 * curl for c, curl in enumerate((c0, c1, c2))]
    for c in range(3):
        h[c, xs, rows] = new[c]


def update_e(e, h, k, j, amp, x, planes, row, n):
    lane = lax.broadcasted_iota(jnp.int32, (planes, n, NZ), 2)
    xs, behind, rows, down = pl.ds(x, planes), pl.ds(x - 1, planes), pl.ds(row, n), pl.ds(row - 1, n)
    krows = pl.ds(row - 8, n)
    h0, h1, h2 = (h[c, xs, rows] for c in range(3))
    c0 = (h2 - h[2, xs, down]) - (h1 - before_z(h1, lane))
    c1 = (h0 - before_z(h0, lane)) - (h2 - h[2, behind, rows])
    c2 = (h1 - h[1, behind, rows]) - (h0 - h[0, xs, down])
    xx, yy, zz, xy, xz, yz = (k[c, xs, krows] for c in range(6))
    new0 = e[0, xs, rows] + ((xx * c0 + xy * c1) + (xz * c2 - amp * j[0, xs, krows]))
    new1 = e[1, xs, rows] + ((xy * c0 + yy * c1) + (yz * c2 - amp * j[1, xs, krows]))
    new2 = e[2, xs, rows] + ((xz * c0 + yz * c1) + (zz * c2 - amp * j[2, xs, krows]))
    for c, new in enumerate((new0, new1, new2)):
        e[c, xs, rows] = new


def kernel(e_in, m_in, ids_in, table, e_out, m_out, et, ht, ef, hf, kk, jj, ids, own_x, own_y, ring, total, amps, *rest):
    out, inn = rest[:8], rest[8:16]
    out_sem, in_sem, id_out, id_in, local = rest[16:]
    gx, gy = lax.axis_index("gx"), lax.axis_index("gy")
    last_x, last_y = lax.axis_size("gx") - 1, lax.axis_size("gy") - 1

    def there(d):
        dx, dy = DIRS[d]
        checks = []
        if dx:
            checks.append(gx > 0 if dx < 0 else gx < last_x)
        if dy:
            checks.append(gy > 0 if dy < 0 else gy < last_y)
        return functools.reduce(jnp.logical_and, checks)

    def device(d):
        return (gx + DIRS[d][0], gy + DIRS[d][1])

    box = (pl.ds(PX, NX), pl.ds(PY, NY))

    def load(i):
        pairs = [(ids_in, ids.at[pl.ds(PX, NX), pl.ds(8, NY)])]
        for comp in range(3):
            pairs.append((e_in.at[comp], et.at[(comp, *box)]))
            pairs.append((m_in.at[comp], ht.at[(comp, *box)]))
        return pltpu.make_async_copy(*pairs[i], local.at[i])

    for i in range(7):
        load(i).start()
    def clear_pieces(slot, c):
        for d in range(8):
            mid, tiles = MID[d], TILES[d]
            inn[d][slot, pl.ds(mid, tiles - mid)] = jnp.zeros((tiles - mid, 8, NZ), jnp.float32)
        return c

    lax.fori_loop(0, SLOTS, clear_pieces, 0)
    barrier = pltpu.get_barrier_semaphore()
    for d in range(8):
        @pl.when(there(d))
        def _(d=d):
            pl.semaphore_signal(barrier, inc=1, device_id=device(d), device_id_type=MESH)
    def around(d):
        dx, dy = DIRS[d]
        xd = pl.ds(PX + NX if dx < 0 else PX - IDS, IDS) if dx else pl.ds(PX, NX)
        yd = pl.ds(8 + NY if dy < 0 else 8 - IDS, IDS) if dy else pl.ds(8, NY)
        return xd, yd

    def id_copy(d):
        xd, yd = around(d)
        dx, dy = DIRS[d]
        xs = pl.ds(0 if dx < 0 else NX - IDS, IDS) if dx else pl.ds(0, NX)
        ys = pl.ds(0 if dy < 0 else NY - IDS, IDS) if dy else pl.ds(0, NY)
        return pltpu.make_async_remote_copy(
            src_ref=ids_in.at[xs, ys],
            dst_ref=ids.at[xd, yd],
            send_sem=id_out.at[d],
            recv_sem=id_in.at[d],
            device_id=device(d),
            device_id_type=MESH,
        )

    for d in range(8):
        @pl.when(jnp.logical_not(there(OPPOSITE[d])))
        def _(d=d):
            xd, yd = around(d)
            ids[xd, yd] = jnp.full((xd.size, yd.size, NZ), -1, jnp.int32)

            if MID[d]:
                def clear(s, c):
                    inn[d][s, pl.ds(0, MID[d])] = jnp.zeros((MID[d], 8, NZ), jnp.float32)
                    return c

                lax.fori_loop(0, SLOTS, clear, 0)

    def clear_planes(x, c):
        for comp in range(3):
            jj[comp, x] = jnp.zeros((YP - 16, NZ), jnp.float32)
            for a in (ef, hf):
                a[comp, x] = jnp.zeros((YP, NZ), jnp.float32)
        return c

    lax.fori_loop(0, XP, clear_planes, 0)
    for step in range(STEPS):
        amps[step] = np.float32(np.sin(np.float32(0.3 * (step + 1))))

    def parts_h(d, depth):
        mid, pieces = MID[d], []
        before, less = pl.ds(DEEP - depth, depth), pl.ds(0, depth - 1)
        if d in (E, N):
            pieces.append((pl.ds(0, mid), pl.ds(0, 8)))
        if d in (W, S, NW, SE):
            pieces.append((pl.ds(mid, 2), before))
        if d in (E, N, NE) and depth > 1:
            pieces.append((pl.ds(mid, 4 if d == NE else 2), less))
        return pieces

    def parts_e(d, depth):
        mid, pieces = MID[d], []
        before, after = pl.ds(DEEP - depth, depth), pl.ds(0, depth)
        if d in (W, S):
            pieces.append((pl.ds(0, mid), pl.ds(0, 8)))
        if depth and d != NE:
            pieces.append((pl.ds(0, 4) if d == SW else pl.ds(mid + 2, 2), before if d in (W, S, SW) else after))
        return pieces

    def parts(d, depth, last):
        return (parts_h(d, depth) if depth else []) + ([] if last else parts_e(d, depth))

    def rows_of(d, depth, last):
        return sum(ts.size * rows.size for ts, rows in parts(d, depth, last))

    def start(slot, depth, some):
        for d in range(8):
            if some(d, depth):
                @pl.when(there(d))
                def _(d=d):
                    for ts, rows in some(d, depth):
                        pltpu.make_async_remote_copy(
                            src_ref=out[d].at[slot, ts, rows],
                            dst_ref=inn[d].at[slot, ts, rows],
                            send_sem=out_sem.at[d],
                            recv_sem=in_sem.at[d, slot],
                            device_id=device(d),
                            device_id_type=MESH,
                        ).start()

    def all_of(rows, sem):
        some = total.at[pl.ds(0, rows)]
        return pltpu.make_async_copy(some, some, sem)

    def arrive(slot, depth, last):
        for d in range(8):
            if parts(d, depth, last):
                @pl.when(there(OPPOSITE[d]))
                def _(d=d):
                    all_of(rows_of(d, depth, last), in_sem.at[d, slot]).wait()

    def leave():
        for d in range(8):
            @pl.when(there(d))
            def _(d=d):
                rows = 0
                for size in SIZES:
                    rows += sum(rows_of(d, m, m == size) for m in range(size + 1))
                all_of(rows, out_sem.at[d]).wait()

    def one_of(depths, do, slot, depth, *what):
        for m in depths:
            @pl.when(depth == m)
            def _(m=m):
                do(slot, m, *what)

    XA, XZ, YA, YZ = PX, PX + NX - 1, PY, PY + NY - 1

    def put_face(d, slot, at, a, comps, x):
        for i, c in enumerate(comps):
            out[d][slot, pl.ds(at + 4 * i, 4)] = a[c, x, pl.ds(YA, NY)].reshape(4, 8, NZ)

    def put_line(d, slot, at, a, comps, y):
        for i, c in enumerate(comps):
            out[d][slot, pl.ds(at + 2 * i, 2)] = a[c, pl.ds(XA, NX), y].reshape(2, 8, NZ)

    def put_piece_y(d, slot, at, a, x, top):
        for i, c in enumerate((1, 2)):
            out[d][slot, at + i] = a[c, x, pl.ds(YZ + 1 if top else YA - DEEP, 8)]

    def put_piece_x(d, slot, at, a, y, right):
        for i, c in enumerate((0, 2)):
            out[d][slot, at + i, pl.ds(0, DEEP)] = a[c, pl.ds(XZ + 1 if right else XA - DEEP, DEEP), y]

    def pack_first(slot):
        put_face(W, slot, 0, et, (1, 2), XA)
        put_line(S, slot, 0, et, (0, 2), YA)
        own_x[slot, pl.ds(2, 2)] = jnp.zeros((2, NY, NZ), jnp.float32)
        own_y[slot, pl.ds(2, 2)] = jnp.zeros((2, NX, NZ), jnp.float32)

    def pack_e(slot):
        put_face(W, slot, 0, ef, (1, 2), XA)
        put_line(S, slot, 0, ef, (0, 2), YA)
        for i, c in enumerate((1, 2)):
            own_x[slot, 2 + i] = ef[c, XZ + 1, pl.ds(YA, NY)]
        for i, c in enumerate((0, 2)):
            own_y[slot, 2 + i] = ef[c, pl.ds(XA, NX), YZ + 1]
        put_piece_x(W, slot, 10, ef, YZ + 1, False)
        put_piece_x(E, slot, 10, ef, YZ + 1, True)
        put_piece_y(S, slot, 6, ef, XZ + 1, False)
        put_piece_y(N, slot, 6, ef, XZ + 1, True)
        put_piece_y(NW, slot, 2, ef, XA, True)
        put_piece_y(SW, slot, 0, ef, XA, False)
        put_piece_x(SW, slot, 2, ef, YA, False)
        put_piece_x(SE, slot, 2, ef, YA, True)

    def pack_h(slot):
        put_face(E, slot, 0, hf, (1, 2), XZ)
        put_line(N, slot, 0, hf, (0, 2), YZ)
        for i, c in enumerate((1, 2)):
            own_x[slot, i] = hf[c, XA - 1, pl.ds(YA, NY)]
        for i, c in enumerate((0, 2)):
            own_y[slot, i] = hf[c, pl.ds(XA, NX), YA - 1]
        put_piece_x(W, slot, 8, hf, YA - 1, False)
        put_piece_x(E, slot, 8, hf, YA - 1, True)
        put_piece_y(S, slot, 4, hf, XA - 1, False)
        put_piece_y(N, slot, 4, hf, XA - 1, True)
        put_piece_x(NW, slot, 0, hf, YZ, False)
        put_piece_y(NE, slot, 0, hf, XZ, True)
        put_piece_x(NE, slot, 2, hf, YZ, True)
        put_piece_y(SE, slot, 0, hf, XZ, False)

    def ring_x(a, x, slot, own, face, low, high):
        for i, c in enumerate((1, 2)):
            d, at = face
            a[c, x, pl.ds(YA, NY)] = own_x[slot, own + i] + inn[d][slot, pl.ds(at + 4 * i, 4)].reshape(NY, NZ)
            for pieces, row in ((low, YA), (high, YA + NY - DEEP)):
                (d1, at1), (d2, at2) = pieces
                some = pl.ds(0, DEEP)
                a[c, x, pl.ds(row, DEEP)] += inn[d1][slot, at1 + i, some] + inn[d2][slot, at2 + i, some]

    def ring_y(a, y, slot, own, face, low, high):
        for i, c in enumerate((0, 2)):
            d, at = face
            ring[...] = own_y[slot, own + i] + inn[d][slot, pl.ds(at + 2 * i, 2)].reshape(NX, NZ)
            for pieces, row in ((low, 0), (high, NX - DEEP)):
                (d1, at1), (d2, at2) = pieces
                some = pl.ds(0, DEEP)
                ring[pl.ds(row, DEEP)] += inn[d1][slot, at1 + i, some] + inn[d2][slot, at2 + i, some]
            a[c, pl.ds(XA, NX), y] = ring[...]

    def ring_e(slot):
        ring_x(et, XZ + 1, slot, 2, (W, 0), ((N, 6), (NW, 2)), ((S, 6), (SW, 0)))
        ring_y(et, YZ + 1, slot, 2, (S, 0), ((E, 10), (SE, 2)), ((W, 10), (SW, 2)))

    def ring_h(slot):
        ring_x(ht, XA - 1, slot, 0, (E, 0), ((N, 4), (NE, 0)), ((S, 4), (SE, 0)))
        ring_y(ht, YA - 1, slot, 0, (N, 0), ((E, 8), (NE, 2)), ((W, 8), (NW, 0)))

    def look(x, planes, row, n, source):
        xs, rows = pl.ds(x, planes), pl.ds(row, n)
        here = ids[xs, rows]
        bits = [(here & (1 << b)) != 0 for b in range(3)]
        real = here >= 0

        def pick(c):
            level = [table[m, c] for m in range(MATS)]
            for b in range(3):
                level = [jnp.where(bits[b], level[2 * i + 1], level[2 * i]) for i in range(len(level) // 2)]
            return level[0]

        tensor = [jnp.where(real, 0.45 * pick(c), 0.0) for c in range(6)]
        for c in range(6):
            kk[c, xs, rows] = tensor[c]
        if source:
            xx, yy, zz, xy, xz, yz = tensor
            s0, s1, s2 = (pick(c) for c in (6, 7, 8))
            jj[0, xs, rows] = xx * s0 + xy * s1 + xz * s2
            jj[1, xs, rows] = xy * s0 + yy * s1 + yz * s2
            jj[2, xs, rows] = xz * s0 + yz * s1 + zz * s2

    def look_own(i, c):
        look(PX + 2 * i, 2, 8, NY, True)
        return c

    def look_rows(i, c):
        look(PX + 4 * i, 4, 0, 8, False)
        look(PX + 4 * i, 4, 8 + NY, 8, False)
        return c

    def look_planes(i, c):
        look(PX - IDS + i, 1, 0, NY + 16, False)
        look(PX + NX + i, 1, 0, NY + 16, False)
        return c

    def frame(update):
        wide, halo = BLOCK - 1, BLOCK // 2
        update(PX - wide, NX + 2 * wide, 8, 16)
        update(PX - wide, NX + 2 * wide, 40, 16)
        update(PX - halo - 1, halo + BLOCK, 24, 16)
        update(PX + NX - BLOCK, halo + BLOCK, 24, 16)

    def lines_h(update):
        update(PX - BLOCK, NX + 2 * BLOCK, 8, 8)
        update(PX - BLOCK, NX + 2 * BLOCK, 40, 8)
        for x in (PX - 1, PX + NX - 1):
            update(x, 1, 16, 24)
            update(x, 1, 48, 8)

    def copy_in(i, c):
        xs, rows = pl.ds(PX + 4 * i, 4), pl.ds(PY, NY)
        for comp in range(3):
            for a, t in ((ef, et), (hf, ht)):
                a[comp, xs, rows] = t[comp, xs, rows]
        return c

    def clean_rows(i, c):
        for comp in range(3):
            for a in (ef, hf):
                for row in (8, PY + NY):
                    a[comp, pl.ds(PX + 4 * i, 4), pl.ds(row, 8)] = jnp.zeros((4, 8, NZ), jnp.float32)
        return c

    def clean_plane(x, c):
        for comp in range(3):
            for a in (ef, hf):
                for at in (x, x + PX + NX):
                    a[comp, at, pl.ds(8, NY + 16)] = jnp.zeros((NY + 16, NZ), jnp.float32)
        return c

    def clean():
        lax.fori_loop(0, NX // 4, clean_rows, 0)
        lax.fori_loop(0, PX, clean_plane, 0)

    def edges_h():
        @pl.when(gx == 0)
        def _():
            for comp in range(3):
                hf[comp, PX - 1, pl.ds(8, NY + 16)] = jnp.zeros((NY + 16, NZ), jnp.float32)

        @pl.when(gy == 0)
        def _():
            for comp in range(3):
                hf[comp, :, pl.ds(8, 8)] = jnp.zeros((XP, 8, NZ), jnp.float32)

    def true_step(step, slot, wait):
        some_e = functools.partial(update_e, et, ht, kk, jj, amps[step])
        ring_e(slot - 1)
        update_h(et, ht, PX, NX, PY, NY)
        some_e(PX + 1, NX - 1, PY + 8, NY - 8)
        wait()
        ring_h(slot)
        some_e(PX, 1, PY, NY)
        some_e(PX + 1, NX - 1, PY, 8)

    load(0).wait()
    lax.fori_loop(0, NX // 2, look_own, 0)
    for i in range(1, 7):
        load(i).wait()
    lax.fori_loop(0, NX // 4, copy_in, 0)
    pack_first(0)
    lines_h(functools.partial(update_h, ef, hf))
    edges_h()
    pack_h(1)
    peers = sum(there(d).astype(jnp.int32) for d in range(8))
    pl.semaphore_wait(barrier, peers)
    start(0, 0, parts_e)
    start(1, 1, parts_h)
    for d in range(8):
        @pl.when(there(d))
        def _(d=d):
            id_copy(d).start()
    clean()
    arrive(0, 0, False)
    true_step(0, 1, functools.partial(arrive, 1, 1, True))
    def look_around():
        for d in range(8):
            @pl.when(there(OPPOSITE[d]))
            def _(d=d):
                id_copy(d).wait_recv()
        lax.fori_loop(0, NX // 4, look_rows, 0)
        lax.fori_loop(0, IDS, look_planes, 0)

    def block(b, c):
        size, begin, base = 4 + b, 5 * b - 4, 6 * b - 4
        pack_first(base)
        start(base, 0, parts_e)
        lax.fori_loop(0, NX // 4, copy_in, 0)

        def free(t, c):
            frame(functools.partial(update_h, ef, hf))
            edges_h()
            pack_h(base + t)
            one_of(range(1, BLOCK), start, base + t, t, parts_h)

            @pl.when((b == 1) & (t == 1))
            def _():
                look_around()

            frame(functools.partial(update_e, ef, hf, kk, jj, amps[begin + t - 1]))
            pack_e(base + t)
            one_of(range(1, BLOCK), start, base + t, t, parts_e)
            return c

        lax.fori_loop(1, size, free, 0)
        lines_h(functools.partial(update_h, ef, hf))
        edges_h()
        pack_h(base + size)
        one_of((BLOCK - 1, BLOCK), start, base + size, size, parts_h)
        clean()
        arrive(base, 0, False)

        def true(t, c):
            def wait():
                @pl.when(t < size)
                def _():
                    one_of(range(1, BLOCK), arrive, base + t, t, False)

                @pl.when(t == size)
                def _():
                    one_of((BLOCK - 1, BLOCK), arrive, base + t, t, True)

            true_step(begin + t - 1, base + t, wait)
            return c

        lax.fori_loop(1, size + 1, true, 0)
        return c

    lax.fori_loop(1, 3, block, 0)

    def stores():
        pairs = [(a.at[(comp, *box)], o.at[comp]) for a, o in ((et, e_out), (ht, m_out)) for comp in range(3)]
        return [pltpu.make_async_copy(src, dst, local.at[1 + i]) for i, (src, dst) in enumerate(pairs)]

    for copy in stores():
        copy.start()

    for d in range(8):
        @pl.when(there(d))
        def _(d=d):
            id_copy(d).wait_send()

    leave()
    for copy in stores():
        copy.wait()


def hand_over(e_in, m_in, e_out, m_out, held, in_sem, out_sem):
    pairs = [(a.at[c], o.at[c]) for a, o in ((e_in, e_out), (m_in, m_out)) for c in range(3)]
    loads = [pltpu.make_async_copy(a, held.at[i], in_sem.at[i]) for i, (a, _) in enumerate(pairs)]
    stores = [pltpu.make_async_copy(held.at[i], o, out_sem.at[i]) for i, (_, o) in enumerate(pairs)]
    for load in loads:
        load.start()
    for load, store in zip(loads, stores):
        load.wait()
        store.start()
    for store in stores:
        store.wait()


def shards(electric, magnetic, material_ids, material_table):
    field = jax.ShapeDtypeStruct((3, NX, NY, NZ), jnp.float32)
    hbm = pl.BlockSpec(memory_space=pl.ANY)
    big = pltpu.VMEM((3, XP, YP, NZ), jnp.float32)
    messages = [pltpu.VMEM((SLOTS, TILES[d], 8, NZ), jnp.float32) for d in range(8)]
    e, m = pl.pallas_call(
        kernel,
        out_shape=(field, field),
        in_specs=[hbm, hbm, hbm, pl.BlockSpec(memory_space=pltpu.SMEM)],
        out_specs=(hbm, hbm),
        scratch_shapes=[
            big,
            big,
            big,
            big,
            pltpu.VMEM((6, XP, YP - 16, NZ), jnp.float32),
            pltpu.VMEM((3, XP, YP - 16, NZ), jnp.float32),
            pltpu.VMEM((XP, YP - 16, NZ), jnp.int32),
            pltpu.VMEM((SLOTS, 4, NY, NZ), jnp.float32),
            pltpu.VMEM((SLOTS, 4, NX, NZ), jnp.float32),
            pltpu.VMEM((NX, NZ), jnp.float32),
            pltpu.VMEM((2048, NZ), jnp.float32),
            pltpu.SMEM((STEPS,), jnp.float32),
            *messages,
            *messages,
            pltpu.SemaphoreType.DMA((8,)),
            pltpu.SemaphoreType.DMA((8, SLOTS)),
            pltpu.SemaphoreType.DMA((8,)),
            pltpu.SemaphoreType.DMA((8,)),
            pltpu.SemaphoreType.DMA((7,)),
        ],
        compiler_params=pltpu.CompilerParams(
            collective_id=0, has_side_effects=True, vmem_limit_bytes=56 * 1024 * 1024
        ),
    )(electric, magnetic, material_ids, material_table)
    return pl.pallas_call(
        hand_over,
        out_shape=(field, field),
        in_specs=[hbm, hbm],
        out_specs=(hbm, hbm),
        scratch_shapes=[pltpu.VMEM((6, NX, NY, NZ), jnp.float32), pltpu.SemaphoreType.DMA((6,)), pltpu.SemaphoreType.DMA((6,))],
    )(e, m)


def solution(mesh):
    placed = (P(None, "gx", "gy", None), P(None, "gx", "gy", None), P("gx", "gy", None), P())
    return jax.shard_map(
        shards,
        mesh=mesh,
        in_specs=placed,
        out_specs=(P(None, "gx", "gy", None), P(None, "gx", "gy", None)),
        check_vma=False,
    )
```

```python
import functools

import jax
import jax.numpy as jnp
import numpy as np
from jax import lax
from jax.experimental import pallas as pl
from jax.experimental.pallas import tpu as pltpu
from jax.sharding import PartitionSpec as P

STEPS = 12
MATS = 8
BLOCK = 4
MESH = pl.DeviceIdType.MESH
NX, NY, NZ = 16, 32, 128
PX = BLOCK + 1
PY = 16
XP, YP = NX + 2 * PX, NY + 2 * PY
DEEP = BLOCK
IDS = BLOCK - 1
SIZES = (1, 3, 4, 4)
SLOTS = 2 + 4 + 5 + 5
TURNS = 2 * (BLOCK + 1)
DIRS = ((-1, 0), (1, 0), (0, -1), (0, 1), (-1, 1), (1, 1), (-1, -1), (1, -1))
W, E, S, N, NW, NE, SW, SE = range(8)
OPPOSITE = (E, W, N, S, SE, SW, NE, NW)
TILES = (12, 12, 8, 8, 4, 4, 4, 4)
MID = (8, 8, 4, 4, 0, 0, 0, 0)


def after_z(a, lane):
    return jnp.where(lane < NZ - 1, pltpu.roll(a, NZ - 1, 2), 0.0)


def before_z(a, lane):
    return jnp.where(lane > 0, pltpu.roll(a, 1, 2), 0.0)


def update_h(e, h, x, planes, row, n):
    lane = lax.broadcasted_iota(jnp.int32, (planes, n, NZ), 2)
    xs, ahead, rows, up = pl.ds(x, planes), pl.ds(x + 1, planes), pl.ds(row, n), pl.ds(row + 1, n)
    e0, e1, e2 = (e[c, xs, rows] for c in range(3))
    c0 = (e[2, xs, up] - e2) - (after_z(e1, lane) - e1)
    c1 = (after_z(e0, lane) - e0) - (e[2, ahead, rows] - e2)
    c2 = (e[1, ahead, rows] - e1) - (e[0, xs, up] - e0)
    new = [h[c, xs, rows] - 0.45 * curl for c, curl in enumerate((c0, c1, c2))]
    for c in range(3):
        h[c, xs, rows] = new[c]


def update_e(e, h, k, j, amp, x, planes, row, n):
    lane = lax.broadcasted_iota(jnp.int32, (planes, n, NZ), 2)
    xs, behind, rows, down = pl.ds(x, planes), pl.ds(x - 1, planes), pl.ds(row, n), pl.ds(row - 1, n)
    krows = pl.ds(row - 8, n)
    h0, h1, h2 = (h[c, xs, rows] for c in range(3))
    c0 = (h2 - h[2, xs, down]) - (h1 - before_z(h1, lane))
    c1 = (h0 - before_z(h0, lane)) - (h2 - h[2, behind, rows])
    c2 = (h1 - h[1, behind, rows]) - (h0 - h[0, xs, down])
    xx, yy, zz, xy, xz, yz = (k[c, xs, krows] for c in range(6))
    new0 = e[0, xs, rows] + ((xx * c0 + xy * c1) + (xz * c2 - amp * j[0, xs, krows]))
    new1 = e[1, xs, rows] + ((xy * c0 + yy * c1) + (yz * c2 - amp * j[1, xs, krows]))
    new2 = e[2, xs, rows] + ((xz * c0 + yz * c1) + (zz * c2 - amp * j[2, xs, krows]))
    for c, new in enumerate((new0, new1, new2)):
        e[c, xs, rows] = new


def kernel(e_in, m_in, ids_in, table, e_out, m_out, et, ht, ef, hf, kk, jj, ids, own_x, own_y, ring, total, amps, *rest):
    out, inn = rest[:8], rest[8:16]
    out_sem, in_sem, id_out, id_in, local = rest[16:]
    gx, gy = lax.axis_index("gx"), lax.axis_index("gy")
    last_x, last_y = lax.axis_size("gx") - 1, lax.axis_size("gy") - 1

    def there(d):
        dx, dy = DIRS[d]
        checks = []
        if dx:
            checks.append(gx > 0 if dx < 0 else gx < last_x)
        if dy:
            checks.append(gy > 0 if dy < 0 else gy < last_y)
        return functools.reduce(jnp.logical_and, checks)

    def device(d):
        return (gx + DIRS[d][0], gy + DIRS[d][1])

    box = (pl.ds(PX, NX), pl.ds(PY, NY))

    def load(i):
        pairs = [(ids_in, ids.at[pl.ds(PX, NX), pl.ds(8, NY)])]
        for comp in range(3):
            pairs.append((e_in.at[comp], et.at[(comp, *box)]))
            pairs.append((m_in.at[comp], ht.at[(comp, *box)]))
        return pltpu.make_async_copy(*pairs[i], local.at[i])

    for i in range(7):
        load(i).start()
    def clear_pieces(slot, c):
        for d in range(8):
            mid, tiles = MID[d], TILES[d]
            inn[d][slot, pl.ds(mid, tiles - mid)] = jnp.zeros((tiles - mid, 8, NZ), jnp.float32)
        return c

    lax.fori_loop(0, SLOTS, clear_pieces, 0)
    barrier = pltpu.get_barrier_semaphore()
    for d in range(8):
        @pl.when(there(d))
        def _(d=d):
            pl.semaphore_signal(barrier, inc=1, device_id=device(d), device_id_type=MESH)
    def around(d):
        dx, dy = DIRS[d]
        xd = pl.ds(PX + NX if dx < 0 else PX - IDS, IDS) if dx else pl.ds(PX, NX)
        yd = pl.ds(8 + NY if dy < 0 else 8 - IDS, IDS) if dy else pl.ds(8, NY)
        return xd, yd

    def id_copy(d):
        xd, yd = around(d)
        dx, dy = DIRS[d]
        xs = pl.ds(0 if dx < 0 else NX - IDS, IDS) if dx else pl.ds(0, NX)
        ys = pl.ds(0 if dy < 0 else NY - IDS, IDS) if dy else pl.ds(0, NY)
        return pltpu.make_async_remote_copy(
            src_ref=ids_in.at[xs, ys],
            dst_ref=ids.at[xd, yd],
            send_sem=id_out.at[d],
            recv_sem=id_in.at[d],
            device_id=device(d),
            device_id_type=MESH,
        )

    for d in range(8):
        @pl.when(jnp.logical_not(there(OPPOSITE[d])))
        def _(d=d):
            xd, yd = around(d)
            ids[xd, yd] = jnp.full((xd.size, yd.size, NZ), -1, jnp.int32)

            if MID[d]:
                def clear(s, c):
                    inn[d][s, pl.ds(0, MID[d])] = jnp.zeros((MID[d], 8, NZ), jnp.float32)
                    return c

                lax.fori_loop(0, SLOTS, clear, 0)

    def clear_planes(x, c):
        for comp in range(3):
            jj[comp, x] = jnp.zeros((YP - 16, NZ), jnp.float32)
            for a in (ef, hf):
                a[comp, x] = jnp.zeros((YP, NZ), jnp.float32)
        return c

    lax.fori_loop(0, XP, clear_planes, 0)
    for step in range(STEPS):
        amps[step] = np.float32(np.sin(np.float32(0.3 * (step + 1))))

    def parts_h(d, depth):
        mid, pieces = MID[d], []
        before, less = pl.ds(DEEP - depth, depth), pl.ds(0, depth - 1)
        if d in (E, N):
            pieces.append((pl.ds(0, mid), pl.ds(0, 8)))
        if d in (W, S, NW, SE):
            pieces.append((pl.ds(mid, 2), before))
        if d in (E, N, NE) and depth > 1:
            pieces.append((pl.ds(mid, 4 if d == NE else 2), less))
        return pieces

    def parts_e(d, depth):
        mid, pieces = MID[d], []
        before, after = pl.ds(DEEP - depth, depth), pl.ds(0, depth)
        if d in (W, S):
            pieces.append((pl.ds(0, mid), pl.ds(0, 8)))
        if depth and d != NE:
            pieces.append((pl.ds(0, 4) if d == SW else pl.ds(mid + 2, 2), before if d in (W, S, SW) else after))
        return pieces

    def parts(d, depth, last):
        return (parts_h(d, depth) if depth else []) + ([] if last else parts_e(d, depth))

    def rows_of(d, depth, last):
        return sum(ts.size * rows.size for ts, rows in parts(d, depth, last))

    def turn(block, depth):
        return lax.rem(block, 2) * (BLOCK + 1) + depth

    def start(block, slot, depth, some):
        for d in range(8):
            if some(d, depth):
                @pl.when(there(d))
                def _(d=d):
                    for ts, rows in some(d, depth):
                        pltpu.make_async_remote_copy(
                            src_ref=out[d].at[slot, ts, rows],
                            dst_ref=inn[d].at[slot, ts, rows],
                            send_sem=out_sem.at[d],
                            recv_sem=in_sem.at[d, turn(block, depth)],
                            device_id=device(d),
                            device_id_type=MESH,
                        ).start()

    def all_of(rows, sem):
        some = total.at[pl.ds(0, rows)]
        return pltpu.make_async_copy(some, some, sem)

    def arrive(block, slot, depth, last):
        for d in range(8):
            if parts(d, depth, last):
                @pl.when(there(OPPOSITE[d]))
                def _(d=d):
                    all_of(rows_of(d, depth, last), in_sem.at[d, turn(block, depth)]).wait()

    def leave():
        for d in range(8):
            @pl.when(there(d))
            def _(d=d):
                rows = 0
                for size in SIZES:
                    rows += sum(rows_of(d, m, m == size) for m in range(size + 1))
                all_of(rows, out_sem.at[d]).wait()

    def one_of(depths, do, block, slot, depth, *what):
        for m in depths:
            @pl.when(depth == m)
            def _(m=m):
                do(block, slot, m, *what)

    XA, XZ, YA, YZ = PX, PX + NX - 1, PY, PY + NY - 1

    def put_face(d, slot, at, a, comps, x):
        for i, c in enumerate(comps):
            out[d][slot, pl.ds(at + 4 * i, 4)] = a[c, x, pl.ds(YA, NY)].reshape(4, 8, NZ)

    def put_line(d, slot, at, a, comps, y):
        for i, c in enumerate(comps):
            out[d][slot, pl.ds(at + 2 * i, 2)] = a[c, pl.ds(XA, NX), y].reshape(2, 8, NZ)

    def put_piece_y(d, slot, at, a, x, top):
        for i, c in enumerate((1, 2)):
            out[d][slot, at + i] = a[c, x, pl.ds(YZ + 1 if top else YA - DEEP, 8)]

    def put_piece_x(d, slot, at, a, y, right):
        for i, c in enumerate((0, 2)):
            out[d][slot, at + i, pl.ds(0, DEEP)] = a[c, pl.ds(XZ + 1 if right else XA - DEEP, DEEP), y]

    def pack_first(slot):
        put_face(W, slot, 0, et, (1, 2), XA)
        put_line(S, slot, 0, et, (0, 2), YA)
        own_x[slot, pl.ds(2, 2)] = jnp.zeros((2, NY, NZ), jnp.float32)
        own_y[slot, pl.ds(2, 2)] = jnp.zeros((2, NX, NZ), jnp.float32)

    def pack_e(slot):
        put_face(W, slot, 0, ef, (1, 2), XA)
        put_line(S, slot, 0, ef, (0, 2), YA)
        for i, c in enumerate((1, 2)):
            own_x[slot, 2 + i] = ef[c, XZ + 1, pl.ds(YA, NY)]
        for i, c in enumerate((0, 2)):
            own_y[slot, 2 + i] = ef[c, pl.ds(XA, NX), YZ + 1]
        put_piece_x(W, slot, 10, ef, YZ + 1, False)
        put_piece_x(E, slot, 10, ef, YZ + 1, True)
        put_piece_y(S, slot, 6, ef, XZ + 1, False)
        put_piece_y(N, slot, 6, ef, XZ + 1, True)
        put_piece_y(NW, slot, 2, ef, XA, True)
        put_piece_y(SW, slot, 0, ef, XA, False)
        put_piece_x(SW, slot, 2, ef, YA, False)
        put_piece_x(SE, slot, 2, ef, YA, True)

    def pack_h(slot):
        put_face(E, slot, 0, hf, (1, 2), XZ)
        put_line(N, slot, 0, hf, (0, 2), YZ)
        for i, c in enumerate((1, 2)):
            own_x[slot, i] = hf[c, XA - 1, pl.ds(YA, NY)]
        for i, c in enumerate((0, 2)):
            own_y[slot, i] = hf[c, pl.ds(XA, NX), YA - 1]
        put_piece_x(W, slot, 8, hf, YA - 1, False)
        put_piece_x(E, slot, 8, hf, YA - 1, True)
        put_piece_y(S, slot, 4, hf, XA - 1, False)
        put_piece_y(N, slot, 4, hf, XA - 1, True)
        put_piece_x(NW, slot, 0, hf, YZ, False)
        put_piece_y(NE, slot, 0, hf, XZ, True)
        put_piece_x(NE, slot, 2, hf, YZ, True)
        put_piece_y(SE, slot, 0, hf, XZ, False)

    def ring_x(a, x, slot, own, face, low, high):
        for i, c in enumerate((1, 2)):
            d, at = face
            a[c, x, pl.ds(YA, NY)] = own_x[slot, own + i] + inn[d][slot, pl.ds(at + 4 * i, 4)].reshape(NY, NZ)
            for pieces, row in ((low, YA), (high, YA + NY - DEEP)):
                (d1, at1), (d2, at2) = pieces
                some = pl.ds(0, DEEP)
                a[c, x, pl.ds(row, DEEP)] += inn[d1][slot, at1 + i, some] + inn[d2][slot, at2 + i, some]

    def ring_y(a, y, slot, own, face, low, high):
        for i, c in enumerate((0, 2)):
            d, at = face
            ring[...] = own_y[slot, own + i] + inn[d][slot, pl.ds(at + 2 * i, 2)].reshape(NX, NZ)
            for pieces, row in ((low, 0), (high, NX - DEEP)):
                (d1, at1), (d2, at2) = pieces
                some = pl.ds(0, DEEP)
                ring[pl.ds(row, DEEP)] += inn[d1][slot, at1 + i, some] + inn[d2][slot, at2 + i, some]
            a[c, pl.ds(XA, NX), y] = ring[...]

    def ring_e(slot):
        ring_x(et, XZ + 1, slot, 2, (W, 0), ((N, 6), (NW, 2)), ((S, 6), (SW, 0)))
        ring_y(et, YZ + 1, slot, 2, (S, 0), ((E, 10), (SE, 2)), ((W, 10), (SW, 2)))

    def ring_h(slot):
        ring_x(ht, XA - 1, slot, 0, (E, 0), ((N, 4), (NE, 0)), ((S, 4), (SE, 0)))
        ring_y(ht, YA - 1, slot, 0, (N, 0), ((E, 8), (NE, 2)), ((W, 8), (NW, 0)))

    def look(x, planes, row, n, source):
        xs, rows = pl.ds(x, planes), pl.ds(row, n)
        here = ids[xs, rows]
        bits = [(here & (1 << b)) != 0 for b in range(3)]
        real = here >= 0

        def pick(c):
            level = [table[m, c] for m in range(MATS)]
            for b in range(3):
                level = [jnp.where(bits[b], level[2 * i + 1], level[2 * i]) for i in range(len(level) // 2)]
            return level[0]

        tensor = [jnp.where(real, 0.45 * pick(c), 0.0) for c in range(6)]
        for c in range(6):
            kk[c, xs, rows] = tensor[c]
        if source:
            xx, yy, zz, xy, xz, yz = tensor
            s0, s1, s2 = (pick(c) for c in (6, 7, 8))
            jj[0, xs, rows] = xx * s0 + xy * s1 + xz * s2
            jj[1, xs, rows] = xy * s0 + yy * s1 + yz * s2
            jj[2, xs, rows] = xz * s0 + yz * s1 + zz * s2

    def look_own(i, c):
        look(PX + 2 * i, 2, 8, NY, True)
        return c

    def look_rows(i, c):
        look(PX + 4 * i, 4, 0, 8, False)
        look(PX + 4 * i, 4, 8 + NY, 8, False)
        return c

    def look_planes(i, c):
        look(PX - IDS + i, 1, 0, NY + 16, False)
        look(PX + NX + i, 1, 0, NY + 16, False)
        return c

    def frame(update):
        wide, halo = BLOCK - 1, BLOCK // 2
        update(PX - wide, NX + 2 * wide, 8, 16)
        update(PX - wide, NX + 2 * wide, 40, 16)
        update(PX - halo - 1, halo + BLOCK, 24, 16)
        update(PX + NX - BLOCK, halo + BLOCK, 24, 16)

    def lines_h(update):
        update(PX - BLOCK, NX + 2 * BLOCK, 8, 8)
        update(PX - BLOCK, NX + 2 * BLOCK, 40, 8)
        for x in (PX - 1, PX + NX - 1):
            update(x, 1, 16, 24)
            update(x, 1, 48, 8)

    def copy_in(i, c):
        xs, rows = pl.ds(PX + 4 * i, 4), pl.ds(PY, NY)
        for comp in range(3):
            for a, t in ((ef, et), (hf, ht)):
                a[comp, xs, rows] = t[comp, xs, rows]
        return c

    def clean_rows(i, c):
        for comp in range(3):
            for a in (ef, hf):
                for row in (8, PY + NY):
                    a[comp, pl.ds(PX + 4 * i, 4), pl.ds(row, 8)] = jnp.zeros((4, 8, NZ), jnp.float32)
        return c

    def clean_plane(x, c):
        for comp in range(3):
            for a in (ef, hf):
                for at in (x, x + PX + NX):
                    a[comp, at, pl.ds(8, NY + 16)] = jnp.zeros((NY + 16, NZ), jnp.float32)
        return c

    def clean():
        lax.fori_loop(0, NX // 4, clean_rows, 0)
        lax.fori_loop(0, PX, clean_plane, 0)

    def edges_h():
        @pl.when(gx == 0)
        def _():
            for comp in range(3):
                hf[comp, PX - 1, pl.ds(8, NY + 16)] = jnp.zeros((NY + 16, NZ), jnp.float32)

        @pl.when(gy == 0)
        def _():
            for comp in range(3):
                hf[comp, :, pl.ds(8, 8)] = jnp.zeros((XP, 8, NZ), jnp.float32)

    def true_step(step, slot, wait, early=lambda: None):
        some_e = functools.partial(update_e, et, ht, kk, jj, amps[step])
        ring_e(slot - 1)
        update_h(et, ht, PX, NX, PY, NY)
        some_e(PX + 1, NX - 1, PY + 8, NY - 8)
        early()
        wait()
        ring_h(slot)
        some_e(PX, 1, PY, NY)
        some_e(PX + 1, NX - 1, PY, 8)

    def stores():
        pairs = [(a.at[(comp, *box)], o.at[comp]) for a, o in ((et, e_out), (ht, m_out)) for comp in range(3)]
        return [pltpu.make_async_copy(src, dst, local.at[1 + i]) for i, (src, dst) in enumerate(pairs)]

    load(0).wait()
    lax.fori_loop(0, NX // 2, look_own, 0)
    for i in range(1, 7):
        load(i).wait()
    lax.fori_loop(0, NX // 4, copy_in, 0)
    pack_first(0)
    lines_h(functools.partial(update_h, ef, hf))
    edges_h()
    pack_h(1)
    peers = sum(there(d).astype(jnp.int32) for d in range(8))
    pl.semaphore_wait(barrier, peers)
    start(0, 0, 0, parts_e)
    start(0, 1, 1, parts_h)
    for d in range(8):
        @pl.when(there(d))
        def _(d=d):
            id_copy(d).start()
    clean()
    arrive(0, 0, 0, False)
    true_step(0, 1, functools.partial(arrive, 0, 1, 1, True))
    def look_around():
        for d in range(8):
            @pl.when(there(OPPOSITE[d]))
            def _(d=d):
                id_copy(d).wait_recv()
        lax.fori_loop(0, NX // 4, look_rows, 0)
        lax.fori_loop(0, IDS, look_planes, 0)

    def block(b, c):
        first = lax.div(1, b)
        size, begin, base = 4 - first, 4 * b - 4 + first, 5 * b - 4 + first
        pack_first(base)
        start(b, base, 0, parts_e)
        lax.fori_loop(0, NX // 4, copy_in, 0)

        def free(t, c):
            frame(functools.partial(update_h, ef, hf))
            edges_h()
            pack_h(base + t)
            one_of(range(1, BLOCK), start, b, base + t, t, parts_h)

            @pl.when((b == 1) & (t == 1))
            def _():
                look_around()

            frame(functools.partial(update_e, ef, hf, kk, jj, amps[begin + t - 1]))
            pack_e(base + t)
            one_of(range(1, BLOCK), start, b, base + t, t, parts_e)
            return c

        lax.fori_loop(1, size, free, 0)
        lines_h(functools.partial(update_h, ef, hf))
        edges_h()
        pack_h(base + size)
        one_of((BLOCK - 1, BLOCK), start, b, base + size, size, parts_h)
        clean()
        arrive(b, base, 0, False)

        def true(t, c):
            def wait():
                @pl.when(t < size)
                def _():
                    one_of(range(1, BLOCK), arrive, b, base + t, t, False)

                @pl.when(t == size)
                def _():
                    one_of((BLOCK - 1, BLOCK), arrive, b, base + t, t, True)

            def early():
                @pl.when(begin + t == STEPS)
                def _():
                    for copy in stores()[3:]:
                        copy.start()

            true_step(begin + t - 1, base + t, wait, early)
            return c

        lax.fori_loop(1, size + 1, true, 0)
        return c

    lax.fori_loop(1, 4, block, 0)

    for copy in stores()[:3]:
        copy.start()

    for d in range(8):
        @pl.when(there(d))
        def _(d=d):
            id_copy(d).wait_send()

    leave()
    for copy in stores():
        copy.wait()


def hand_over(e_in, m_in, e_out, m_out, held, in_sem, out_sem):
    pairs = [(a.at[c], o.at[c]) for a, o in ((e_in, e_out), (m_in, m_out)) for c in range(3)]
    loads = [pltpu.make_async_copy(a, held.at[i], in_sem.at[i]) for i, (a, _) in enumerate(pairs)]
    stores = [pltpu.make_async_copy(held.at[i], o, out_sem.at[i]) for i, (_, o) in enumerate(pairs)]
    for load in loads:
        load.start()
    for load, store in zip(loads, stores):
        load.wait()
        store.start()
    for store in stores:
        store.wait()


def shards(electric, magnetic, material_ids, material_table):
    field = jax.ShapeDtypeStruct((3, NX, NY, NZ), jnp.float32)
    hbm = pl.BlockSpec(memory_space=pl.ANY)
    big = pltpu.VMEM((3, XP, YP, NZ), jnp.float32)
    messages = [pltpu.VMEM((SLOTS, TILES[d], 8, NZ), jnp.float32) for d in range(8)]
    e, m = pl.pallas_call(
        kernel,
        out_shape=(field, field),
        in_specs=[hbm, hbm, hbm, pl.BlockSpec(memory_space=pltpu.SMEM)],
        out_specs=(hbm, hbm),
        scratch_shapes=[
            big,
            big,
            big,
            big,
            pltpu.VMEM((6, XP, YP - 16, NZ), jnp.float32),
            pltpu.VMEM((3, XP, YP - 16, NZ), jnp.float32),
            pltpu.VMEM((XP, YP - 16, NZ), jnp.int32),
            pltpu.VMEM((SLOTS, 4, NY, NZ), jnp.float32),
            pltpu.VMEM((SLOTS, 4, NX, NZ), jnp.float32),
            pltpu.VMEM((NX, NZ), jnp.float32),
            pltpu.VMEM((2048, NZ), jnp.float32),
            pltpu.SMEM((STEPS,), jnp.float32),
            *messages,
            *messages,
            pltpu.SemaphoreType.DMA((8,)),
            pltpu.SemaphoreType.DMA((8, TURNS)),
            pltpu.SemaphoreType.DMA((8,)),
            pltpu.SemaphoreType.DMA((8,)),
            pltpu.SemaphoreType.DMA((7,)),
        ],
        compiler_params=pltpu.CompilerParams(
            collective_id=0, has_side_effects=True, vmem_limit_bytes=56 * 1024 * 1024
        ),
    )(electric, magnetic, material_ids, material_table)
    return pl.pallas_call(
        hand_over,
        out_shape=(field, field),
        in_specs=[hbm, hbm],
        out_specs=(hbm, hbm),
        scratch_shapes=[pltpu.VMEM((6, NX, NY, NZ), jnp.float32), pltpu.SemaphoreType.DMA((6,)), pltpu.SemaphoreType.DMA((6,))],
    )(e, m)


def solution(mesh):
    placed = (P(None, "gx", "gy", None), P(None, "gx", "gy", None), P("gx", "gy", None), P())
    return jax.shard_map(
        shards,
        mesh=mesh,
        in_specs=placed,
        out_specs=(P(None, "gx", "gy", None), P(None, "gx", "gy", None)),
        check_vma=False,
    )
```

```python
import functools

import jax
import jax.numpy as jnp
import numpy as np
from jax import lax
from jax.experimental import pallas as pl
from jax.experimental.pallas import tpu as pltpu
from jax.sharding import PartitionSpec as P

STEPS = 12
MATS = 8
BLOCK = 4
MESH = pl.DeviceIdType.MESH
NX, NY, NZ = 16, 32, 128
PX = BLOCK + 1
PY = 16
XP, YP = NX + 2 * PX, NY + 2 * PY
DEEP = BLOCK
IDS = BLOCK - 1
SIZES = (1, 3, 4, 4)
SLOTS = 2 + 4 + 5 + 5
TURNS = 2 * (BLOCK + 1)
DIRS = ((-1, 0), (1, 0), (0, -1), (0, 1), (-1, 1), (1, 1), (-1, -1), (1, -1))
W, E, S, N, NW, NE, SW, SE = range(8)
OPPOSITE = (E, W, N, S, SE, SW, NE, NW)
TILES = (12, 12, 8, 8, 4, 4, 4, 4)
MID = (8, 8, 4, 4, 0, 0, 0, 0)


def after_z(a, lane):
    return jnp.where(lane < NZ - 1, pltpu.roll(a, NZ - 1, 2), 0.0)


def before_z(a, lane):
    return jnp.where(lane > 0, pltpu.roll(a, 1, 2), 0.0)


def update_h(e, h, x, planes, row, n):
    lane = lax.broadcasted_iota(jnp.int32, (planes, n, NZ), 2)
    xs, ahead, rows, up = pl.ds(x, planes), pl.ds(x + 1, planes), pl.ds(row, n), pl.ds(row + 1, n)
    e0, e1, e2 = (e[c, xs, rows] for c in range(3))
    c0 = (e[2, xs, up] - e2) - (after_z(e1, lane) - e1)
    c1 = (after_z(e0, lane) - e0) - (e[2, ahead, rows] - e2)
    c2 = (e[1, ahead, rows] - e1) - (e[0, xs, up] - e0)
    new = [h[c, xs, rows] - 0.45 * curl for c, curl in enumerate((c0, c1, c2))]
    for c in range(3):
        h[c, xs, rows] = new[c]


def update_e(e, h, k, j, amp, x, planes, row, n):
    lane = lax.broadcasted_iota(jnp.int32, (planes, n, NZ), 2)
    xs, behind, rows, down = pl.ds(x, planes), pl.ds(x - 1, planes), pl.ds(row, n), pl.ds(row - 1, n)
    krows = pl.ds(row - 8, n)
    h0, h1, h2 = (h[c, xs, rows] for c in range(3))
    c0 = (h2 - h[2, xs, down]) - (h1 - before_z(h1, lane))
    c1 = (h0 - before_z(h0, lane)) - (h2 - h[2, behind, rows])
    c2 = (h1 - h[1, behind, rows]) - (h0 - h[0, xs, down])
    xx, yy, zz, xy, xz, yz = (k[c, xs, krows] for c in range(6))
    new0 = e[0, xs, rows] + ((xx * c0 + xy * c1) + (xz * c2 - amp * j[0, xs, krows]))
    new1 = e[1, xs, rows] + ((xy * c0 + yy * c1) + (yz * c2 - amp * j[1, xs, krows]))
    new2 = e[2, xs, rows] + ((xz * c0 + yz * c1) + (zz * c2 - amp * j[2, xs, krows]))
    for c, new in enumerate((new0, new1, new2)):
        e[c, xs, rows] = new


def kernel(e_in, m_in, ids_in, table, e_out, m_out, et, ht, ef, hf, kk, jj, ids, own_x, own_y, ring, total, amps, *rest):
    out, inn = rest[:8], rest[8:16]
    out_sem, in_sem, id_out, id_in, local = rest[16:]
    gx, gy = lax.axis_index("gx"), lax.axis_index("gy")
    last_x, last_y = lax.axis_size("gx") - 1, lax.axis_size("gy") - 1

    def there(d):
        dx, dy = DIRS[d]
        checks = []
        if dx:
            checks.append(gx > 0 if dx < 0 else gx < last_x)
        if dy:
            checks.append(gy > 0 if dy < 0 else gy < last_y)
        return functools.reduce(jnp.logical_and, checks)

    def device(d):
        return (gx + DIRS[d][0], gy + DIRS[d][1])

    box = (pl.ds(PX, NX), pl.ds(PY, NY))

    def load(i):
        pairs = [(ids_in, ids.at[pl.ds(PX, NX), pl.ds(8, NY)])]
        for comp in range(3):
            pairs.append((e_in.at[comp], et.at[(comp, *box)]))
            pairs.append((m_in.at[comp], ht.at[(comp, *box)]))
        return pltpu.make_async_copy(*pairs[i], local.at[i])

    for i in range(7):
        load(i).start()
    def clear_pieces(slot, c):
        for d in range(8):
            mid, tiles = MID[d], TILES[d]
            inn[d][slot, pl.ds(mid, tiles - mid)] = jnp.zeros((tiles - mid, 8, NZ), jnp.float32)
        return c

    lax.fori_loop(0, SLOTS, clear_pieces, 0)
    barrier = pltpu.get_barrier_semaphore()
    for d in range(8):
        @pl.when(there(d))
        def _(d=d):
            pl.semaphore_signal(barrier, inc=1, device_id=device(d), device_id_type=MESH)
    def around(d):
        dx, dy = DIRS[d]
        xd = pl.ds(PX + NX if dx < 0 else PX - IDS, IDS) if dx else pl.ds(PX, NX)
        yd = pl.ds(8 + NY if dy < 0 else 8 - IDS, IDS) if dy else pl.ds(8, NY)
        return xd, yd

    def id_copy(d):
        xd, yd = around(d)
        dx, dy = DIRS[d]
        xs = pl.ds(0 if dx < 0 else NX - IDS, IDS) if dx else pl.ds(0, NX)
        ys = pl.ds(0 if dy < 0 else NY - IDS, IDS) if dy else pl.ds(0, NY)
        return pltpu.make_async_remote_copy(
            src_ref=ids_in.at[xs, ys],
            dst_ref=ids.at[xd, yd],
            send_sem=id_out.at[d],
            recv_sem=id_in.at[d],
            device_id=device(d),
            device_id_type=MESH,
        )

    for d in range(8):
        @pl.when(jnp.logical_not(there(OPPOSITE[d])))
        def _(d=d):
            xd, yd = around(d)
            ids[xd, yd] = jnp.full((xd.size, yd.size, NZ), -1, jnp.int32)

            if MID[d]:
                def clear(s, c):
                    inn[d][s, pl.ds(0, MID[d])] = jnp.zeros((MID[d], 8, NZ), jnp.float32)
                    return c

                lax.fori_loop(0, SLOTS, clear, 0)

    def clear_planes(x, c):
        for comp in range(3):
            jj[comp, x] = jnp.zeros((YP - 16, NZ), jnp.float32)
            for a in (ef, hf):
                a[comp, x] = jnp.zeros((YP, NZ), jnp.float32)
        return c

    lax.fori_loop(0, XP, clear_planes, 0)
    for step in range(STEPS):
        amps[step] = np.float32(np.sin(np.float32(0.3 * (step + 1))))

    def parts_h(d, depth):
        mid, pieces = MID[d], []
        before, less = pl.ds(DEEP - depth, depth), pl.ds(0, depth - 1)
        if d in (E, N):
            pieces.append((pl.ds(0, mid), pl.ds(0, 8)))
        if d in (W, S, NW, SE):
            pieces.append((pl.ds(mid, 2), before))
        if d in (E, N, NE) and depth > 1:
            pieces.append((pl.ds(mid, 4 if d == NE else 2), less))
        return pieces

    def parts_e(d, depth):
        mid, pieces = MID[d], []
        before, after = pl.ds(DEEP - depth, depth), pl.ds(0, depth)
        if d in (W, S):
            pieces.append((pl.ds(0, mid), pl.ds(0, 8)))
        if depth and d != NE:
            pieces.append((pl.ds(0, 4) if d == SW else pl.ds(mid + 2, 2), before if d in (W, S, SW) else after))
        return pieces

    def parts(d, depth, last):
        return (parts_h(d, depth) if depth else []) + ([] if last else parts_e(d, depth))

    def rows_of(d, depth, last):
        return sum(ts.size * rows.size for ts, rows in parts(d, depth, last))

    def turn(block, depth):
        return lax.rem(block, 2) * (BLOCK + 1) + depth

    def start(block, slot, depth, some):
        for d in (N, S, W, E, NW, NE, SW, SE):
            if some(d, depth):
                @pl.when(there(d))
                def _(d=d):
                    for ts, rows in some(d, depth):
                        pltpu.make_async_remote_copy(
                            src_ref=out[d].at[slot, ts, rows],
                            dst_ref=inn[d].at[slot, ts, rows],
                            send_sem=out_sem.at[d],
                            recv_sem=in_sem.at[d, turn(block, depth)],
                            device_id=device(d),
                            device_id_type=MESH,
                        ).start()

    def all_of(rows, sem):
        some = total.at[pl.ds(0, rows)]
        return pltpu.make_async_copy(some, some, sem)

    def arrive(block, slot, depth, last):
        for d in range(8):
            if parts(d, depth, last):
                @pl.when(there(OPPOSITE[d]))
                def _(d=d):
                    all_of(rows_of(d, depth, last), in_sem.at[d, turn(block, depth)]).wait()

    def leave():
        for d in range(8):
            @pl.when(there(d))
            def _(d=d):
                rows = 0
                for size in SIZES:
                    rows += sum(rows_of(d, m, m == size) for m in range(size + 1))
                all_of(rows, out_sem.at[d]).wait()

    def one_of(depths, do, block, slot, depth, *what):
        for m in depths:
            @pl.when(depth == m)
            def _(m=m):
                do(block, slot, m, *what)

    XA, XZ, YA, YZ = PX, PX + NX - 1, PY, PY + NY - 1

    def put_face(d, slot, at, a, comps, x):
        for i, c in enumerate(comps):
            out[d][slot, pl.ds(at + 4 * i, 4)] = a[c, x, pl.ds(YA, NY)].reshape(4, 8, NZ)

    def put_line(d, slot, at, a, comps, y):
        for i, c in enumerate(comps):
            out[d][slot, pl.ds(at + 2 * i, 2)] = a[c, pl.ds(XA, NX), y].reshape(2, 8, NZ)

    def put_piece_y(d, slot, at, a, x, top):
        for i, c in enumerate((1, 2)):
            out[d][slot, at + i] = a[c, x, pl.ds(YZ + 1 if top else YA - DEEP, 8)]

    def put_piece_x(d, slot, at, a, y, right):
        for i, c in enumerate((0, 2)):
            out[d][slot, at + i, pl.ds(0, DEEP)] = a[c, pl.ds(XZ + 1 if right else XA - DEEP, DEEP), y]

    def pack_first(slot):
        put_face(W, slot, 0, et, (1, 2), XA)
        put_line(S, slot, 0, et, (0, 2), YA)
        own_x[slot, pl.ds(2, 2)] = jnp.zeros((2, NY, NZ), jnp.float32)
        own_y[slot, pl.ds(2, 2)] = jnp.zeros((2, NX, NZ), jnp.float32)

    def pack_e(slot):
        put_face(W, slot, 0, ef, (1, 2), XA)
        put_line(S, slot, 0, ef, (0, 2), YA)
        for i, c in enumerate((1, 2)):
            own_x[slot, 2 + i] = ef[c, XZ + 1, pl.ds(YA, NY)]
        for i, c in enumerate((0, 2)):
            own_y[slot, 2 + i] = ef[c, pl.ds(XA, NX), YZ + 1]
        put_piece_x(W, slot, 10, ef, YZ + 1, False)
        put_piece_x(E, slot, 10, ef, YZ + 1, True)
        put_piece_y(S, slot, 6, ef, XZ + 1, False)
        put_piece_y(N, slot, 6, ef, XZ + 1, True)
        put_piece_y(NW, slot, 2, ef, XA, True)
        put_piece_y(SW, slot, 0, ef, XA, False)
        put_piece_x(SW, slot, 2, ef, YA, False)
        put_piece_x(SE, slot, 2, ef, YA, True)

    def pack_h(slot):
        put_face(E, slot, 0, hf, (1, 2), XZ)
        put_line(N, slot, 0, hf, (0, 2), YZ)
        for i, c in enumerate((1, 2)):
            own_x[slot, i] = hf[c, XA - 1, pl.ds(YA, NY)]
        for i, c in enumerate((0, 2)):
            own_y[slot, i] = hf[c, pl.ds(XA, NX), YA - 1]
        put_piece_x(W, slot, 8, hf, YA - 1, False)
        put_piece_x(E, slot, 8, hf, YA - 1, True)
        put_piece_y(S, slot, 4, hf, XA - 1, False)
        put_piece_y(N, slot, 4, hf, XA - 1, True)
        put_piece_x(NW, slot, 0, hf, YZ, False)
        put_piece_y(NE, slot, 0, hf, XZ, True)
        put_piece_x(NE, slot, 2, hf, YZ, True)
        put_piece_y(SE, slot, 0, hf, XZ, False)

    def ring_x(a, x, slot, own, face, low, high):
        for i, c in enumerate((1, 2)):
            d, at = face
            a[c, x, pl.ds(YA, NY)] = own_x[slot, own + i] + inn[d][slot, pl.ds(at + 4 * i, 4)].reshape(NY, NZ)
            for pieces, row in ((low, YA), (high, YA + NY - DEEP)):
                (d1, at1), (d2, at2) = pieces
                some = pl.ds(0, DEEP)
                a[c, x, pl.ds(row, DEEP)] += inn[d1][slot, at1 + i, some] + inn[d2][slot, at2 + i, some]

    def ring_y(a, y, slot, own, face, low, high):
        for i, c in enumerate((0, 2)):
            d, at = face
            ring[...] = own_y[slot, own + i] + inn[d][slot, pl.ds(at + 2 * i, 2)].reshape(NX, NZ)
            for pieces, row in ((low, 0), (high, NX - DEEP)):
                (d1, at1), (d2, at2) = pieces
                some = pl.ds(0, DEEP)
                ring[pl.ds(row, DEEP)] += inn[d1][slot, at1 + i, some] + inn[d2][slot, at2 + i, some]
            a[c, pl.ds(XA, NX), y] = ring[...]

    def ring_e(slot):
        ring_x(et, XZ + 1, slot, 2, (W, 0), ((N, 6), (NW, 2)), ((S, 6), (SW, 0)))
        ring_y(et, YZ + 1, slot, 2, (S, 0), ((E, 10), (SE, 2)), ((W, 10), (SW, 2)))

    def ring_h(slot):
        ring_x(ht, XA - 1, slot, 0, (E, 0), ((N, 4), (NE, 0)), ((S, 4), (SE, 0)))
        ring_y(ht, YA - 1, slot, 0, (N, 0), ((E, 8), (NE, 2)), ((W, 8), (NW, 0)))

    def look(x, planes, row, n, source):
        xs, rows = pl.ds(x, planes), pl.ds(row, n)
        here = ids[xs, rows]
        bits = [(here & (1 << b)) != 0 for b in range(3)]
        real = here >= 0

        def pick(c):
            level = [table[m, c] for m in range(MATS)]
            for b in range(3):
                level = [jnp.where(bits[b], level[2 * i + 1], level[2 * i]) for i in range(len(level) // 2)]
            return level[0]

        tensor = [jnp.where(real, 0.45 * pick(c), 0.0) for c in range(6)]
        for c in range(6):
            kk[c, xs, rows] = tensor[c]
        if source:
            xx, yy, zz, xy, xz, yz = tensor
            s0, s1, s2 = (pick(c) for c in (6, 7, 8))
            jj[0, xs, rows] = xx * s0 + xy * s1 + xz * s2
            jj[1, xs, rows] = xy * s0 + yy * s1 + yz * s2
            jj[2, xs, rows] = xz * s0 + yz * s1 + zz * s2

    def look_own(i, c):
        look(PX + 2 * i, 2, 8, NY, True)
        return c

    def look_rows(i, c):
        look(PX + 4 * i, 4, 0, 8, False)
        look(PX + 4 * i, 4, 8 + NY, 8, False)
        return c

    def look_planes(i, c):
        look(PX - IDS + i, 1, 0, NY + 16, False)
        look(PX + NX + i, 1, 0, NY + 16, False)
        return c

    def frame(update):
        wide, halo = BLOCK - 1, BLOCK // 2
        update(PX - wide, NX + 2 * wide, 8, 16)
        update(PX - wide, NX + 2 * wide, 40, 16)
        update(PX - halo - 1, halo + BLOCK, 24, 16)
        update(PX + NX - BLOCK, halo + BLOCK, 24, 16)

    def lines_h(update):
        update(PX - BLOCK, NX + 2 * BLOCK, 8, 8)
        update(PX - BLOCK, NX + 2 * BLOCK, 40, 8)
        for x in (PX - 1, PX + NX - 1):
            update(x, 1, 16, 24)
            update(x, 1, 48, 8)

    def copy_in(i, c):
        xs, rows = pl.ds(PX + 4 * i, 4), pl.ds(PY, NY)
        for comp in range(3):
            for a, t in ((ef, et), (hf, ht)):
                a[comp, xs, rows] = t[comp, xs, rows]
        return c

    def clean_rows(i, c):
        for comp in range(3):
            for a in (ef, hf):
                for row in (8, PY + NY):
                    a[comp, pl.ds(PX + 4 * i, 4), pl.ds(row, 8)] = jnp.zeros((4, 8, NZ), jnp.float32)
        return c

    def clean_plane(x, c):
        for comp in range(3):
            for a in (ef, hf):
                for at in (x, x + PX + NX):
                    a[comp, at, pl.ds(8, NY + 16)] = jnp.zeros((NY + 16, NZ), jnp.float32)
        return c

    def clean():
        lax.fori_loop(0, NX // 4, clean_rows, 0)
        lax.fori_loop(0, PX, clean_plane, 0)

    def edges_h():
        @pl.when(gx == 0)
        def _():
            for comp in range(3):
                hf[comp, PX - 1, pl.ds(8, NY + 16)] = jnp.zeros((NY + 16, NZ), jnp.float32)

        @pl.when(gy == 0)
        def _():
            for comp in range(3):
                hf[comp, :, pl.ds(8, 8)] = jnp.zeros((XP, 8, NZ), jnp.float32)

    def true_step(step, slot, wait, early=lambda: None):
        some_e = functools.partial(update_e, et, ht, kk, jj, amps[step])
        ring_e(slot - 1)
        update_h(et, ht, PX, NX, PY, NY)
        some_e(PX + 1, NX - 1, PY + 8, NY - 8)
        early()
        wait()
        ring_h(slot)
        some_e(PX, 1, PY, NY)
        some_e(PX + 1, NX - 1, PY, 8)

    def stores():
        pairs = [(a.at[(comp, *box)], o.at[comp]) for a, o in ((et, e_out), (ht, m_out)) for comp in range(3)]
        return [pltpu.make_async_copy(src, dst, local.at[1 + i]) for i, (src, dst) in enumerate(pairs)]

    load(0).wait()
    lax.fori_loop(0, NX // 2, look_own, 0)
    for i in range(1, 7):
        load(i).wait()
    lax.fori_loop(0, NX // 4, copy_in, 0)
    pack_first(0)
    lines_h(functools.partial(update_h, ef, hf))
    edges_h()
    pack_h(1)
    peers = sum(there(d).astype(jnp.int32) for d in range(8))
    pl.semaphore_wait(barrier, peers)
    start(0, 0, 0, parts_e)
    start(0, 1, 1, parts_h)
    for d in range(8):
        @pl.when(there(d))
        def _(d=d):
            id_copy(d).start()
    clean()
    arrive(0, 0, 0, False)
    true_step(0, 1, functools.partial(arrive, 0, 1, 1, True))
    def look_around():
        for d in range(8):
            @pl.when(there(OPPOSITE[d]))
            def _(d=d):
                id_copy(d).wait_recv()
        lax.fori_loop(0, NX // 4, look_rows, 0)
        lax.fori_loop(0, IDS, look_planes, 0)

    def block(b, c):
        first = lax.div(1, b)
        size, begin, base = 4 - first, 4 * b - 4 + first, 5 * b - 4 + first
        pack_first(base)
        start(b, base, 0, parts_e)
        lax.fori_loop(0, NX // 4, copy_in, 0)

        def free(t, c):
            frame(functools.partial(update_h, ef, hf))
            edges_h()
            pack_h(base + t)
            one_of(range(1, BLOCK), start, b, base + t, t, parts_h)

            @pl.when((b == 1) & (t == 1))
            def _():
                look_around()

            frame(functools.partial(update_e, ef, hf, kk, jj, amps[begin + t - 1]))
            pack_e(base + t)
            one_of(range(1, BLOCK), start, b, base + t, t, parts_e)
            return c

        lax.fori_loop(1, size, free, 0)
        lines_h(functools.partial(update_h, ef, hf))
        edges_h()
        pack_h(base + size)
        one_of((BLOCK - 1, BLOCK), start, b, base + size, size, parts_h)
        clean()
        arrive(b, base, 0, False)

        def true(t, c):
            def wait():
                @pl.when(t < size)
                def _():
                    one_of(range(1, BLOCK), arrive, b, base + t, t, False)

                @pl.when(t == size)
                def _():
                    one_of((BLOCK - 1, BLOCK), arrive, b, base + t, t, True)

            def early():
                @pl.when(begin + t == STEPS)
                def _():
                    for copy in stores()[3:]:
                        copy.start()

            true_step(begin + t - 1, base + t, wait, early)
            return c

        lax.fori_loop(1, size + 1, true, 0)
        return c

    lax.fori_loop(1, 4, block, 0)

    for copy in stores()[:3]:
        copy.start()

    for d in range(8):
        @pl.when(there(d))
        def _(d=d):
            id_copy(d).wait_send()

    leave()
    for copy in stores():
        copy.wait()


def hand_over(e_in, m_in, e_out, m_out, held, in_sem, out_sem):
    pairs = [(a.at[c], o.at[c]) for a, o in ((e_in, e_out), (m_in, m_out)) for c in range(3)]
    loads = [pltpu.make_async_copy(a, held.at[i], in_sem.at[i]) for i, (a, _) in enumerate(pairs)]
    stores = [pltpu.make_async_copy(held.at[i], o, out_sem.at[i]) for i, (_, o) in enumerate(pairs)]
    for load in loads:
        load.start()
    for load, store in zip(loads, stores):
        load.wait()
        store.start()
    for store in stores:
        store.wait()


def shards(electric, magnetic, material_ids, material_table):
    field = jax.ShapeDtypeStruct((3, NX, NY, NZ), jnp.float32)
    hbm = pl.BlockSpec(memory_space=pl.ANY)
    big = pltpu.VMEM((3, XP, YP, NZ), jnp.float32)
    messages = [pltpu.VMEM((SLOTS, TILES[d], 8, NZ), jnp.float32) for d in range(8)]
    e, m = pl.pallas_call(
        kernel,
        out_shape=(field, field),
        in_specs=[hbm, hbm, hbm, pl.BlockSpec(memory_space=pltpu.SMEM)],
        out_specs=(hbm, hbm),
        scratch_shapes=[
            big,
            big,
            big,
            big,
            pltpu.VMEM((6, XP, YP - 16, NZ), jnp.float32),
            pltpu.VMEM((3, XP, YP - 16, NZ), jnp.float32),
            pltpu.VMEM((XP, YP - 16, NZ), jnp.int32),
            pltpu.VMEM((SLOTS, 4, NY, NZ), jnp.float32),
            pltpu.VMEM((SLOTS, 4, NX, NZ), jnp.float32),
            pltpu.VMEM((NX, NZ), jnp.float32),
            pltpu.VMEM((2048, NZ), jnp.float32),
            pltpu.SMEM((STEPS,), jnp.float32),
            *messages,
            *messages,
            pltpu.SemaphoreType.DMA((8,)),
            pltpu.SemaphoreType.DMA((8, TURNS)),
            pltpu.SemaphoreType.DMA((8,)),
            pltpu.SemaphoreType.DMA((8,)),
            pltpu.SemaphoreType.DMA((7,)),
        ],
        compiler_params=pltpu.CompilerParams(
            collective_id=0, has_side_effects=True, vmem_limit_bytes=56 * 1024 * 1024
        ),
    )(electric, magnetic, material_ids, material_table)
    return pl.pallas_call(
        hand_over,
        out_shape=(field, field),
        in_specs=[hbm, hbm],
        out_specs=(hbm, hbm),
        scratch_shapes=[pltpu.VMEM((6, NX, NY, NZ), jnp.float32), pltpu.SemaphoreType.DMA((6,)), pltpu.SemaphoreType.DMA((6,))],
    )(e, m)


def solution(mesh):
    placed = (P(None, "gx", "gy", None), P(None, "gx", "gy", None), P("gx", "gy", None), P())
    return jax.shard_map(
        shards,
        mesh=mesh,
        in_specs=placed,
        out_specs=(P(None, "gx", "gy", None), P(None, "gx", "gy", None)),
        check_vma=False,
    )
```

```python
import functools

import jax
import jax.numpy as jnp
import numpy as np
from jax import lax
from jax.experimental import pallas as pl
from jax.experimental.pallas import tpu as pltpu
from jax.sharding import PartitionSpec as P

STEPS = 12
MATS = 8
BLOCK = 4
MESH = pl.DeviceIdType.MESH
NX, NY, NZ = 16, 32, 128
PX = BLOCK + 1
PY = 16
XP, YP = NX + 2 * PX, NY + 2 * PY
DEEP = BLOCK
IDS = BLOCK - 1
SIZES = (1, 3, 4, 4)
SLOTS = 2 + 4 + 5 + 5
TURNS = 2 * (BLOCK + 1)
DIRS = ((-1, 0), (1, 0), (0, -1), (0, 1), (-1, 1), (1, 1), (-1, -1), (1, -1))
W, E, S, N, NW, NE, SW, SE = range(8)
OPPOSITE = (E, W, N, S, SE, SW, NE, NW)
TILES = (12, 12, 8, 8, 4, 4, 4, 4)
MID = (8, 8, 4, 4, 0, 0, 0, 0)


def after_z(a, lane):
    return jnp.where(lane < NZ - 1, pltpu.roll(a, NZ - 1, 2), 0.0)


def before_z(a, lane):
    return jnp.where(lane > 0, pltpu.roll(a, 1, 2), 0.0)


def update_h(e, h, x, planes, row, n):
    lane = lax.broadcasted_iota(jnp.int32, (planes, n, NZ), 2)
    xs, ahead, rows, up = pl.ds(x, planes), pl.ds(x + 1, planes), pl.ds(row, n), pl.ds(row + 1, n)
    e0, e1, e2 = (e[c, xs, rows] for c in range(3))
    c0 = (e[2, xs, up] - e2) - (after_z(e1, lane) - e1)
    c1 = (after_z(e0, lane) - e0) - (e[2, ahead, rows] - e2)
    c2 = (e[1, ahead, rows] - e1) - (e[0, xs, up] - e0)
    new = [h[c, xs, rows] - 0.45 * curl for c, curl in enumerate((c0, c1, c2))]
    for c in range(3):
        h[c, xs, rows] = new[c]


def update_e(e, h, k, j, amp, x, planes, row, n):
    lane = lax.broadcasted_iota(jnp.int32, (planes, n, NZ), 2)
    xs, behind, rows, down = pl.ds(x, planes), pl.ds(x - 1, planes), pl.ds(row, n), pl.ds(row - 1, n)
    krows = pl.ds(row - 8, n)
    h0, h1, h2 = (h[c, xs, rows] for c in range(3))
    c0 = (h2 - h[2, xs, down]) - (h1 - before_z(h1, lane))
    c1 = (h0 - before_z(h0, lane)) - (h2 - h[2, behind, rows])
    c2 = (h1 - h[1, behind, rows]) - (h0 - h[0, xs, down])
    xx, yy, zz, xy, xz, yz = (k[c, xs, krows] for c in range(6))
    new0 = e[0, xs, rows] + ((xx * c0 + xy * c1) + (xz * c2 - amp * j[0, xs, krows]))
    new1 = e[1, xs, rows] + ((xy * c0 + yy * c1) + (yz * c2 - amp * j[1, xs, krows]))
    new2 = e[2, xs, rows] + ((xz * c0 + yz * c1) + (zz * c2 - amp * j[2, xs, krows]))
    for c, new in enumerate((new0, new1, new2)):
        e[c, xs, rows] = new


def kernel(e_in, m_in, ids_in, table, e_out, m_out, et, ht, ef, hf, kk, jj, ids, own_x, own_y, ring, total, amps, *rest):
    out, inn = rest[:8], rest[8:16]
    out_sem, in_sem, id_in, local = rest[16:]
    gx, gy = lax.axis_index("gx"), lax.axis_index("gy")
    last_x, last_y = lax.axis_size("gx") - 1, lax.axis_size("gy") - 1

    def there(d):
        dx, dy = DIRS[d]
        checks = []
        if dx:
            checks.append(gx > 0 if dx < 0 else gx < last_x)
        if dy:
            checks.append(gy > 0 if dy < 0 else gy < last_y)
        return functools.reduce(jnp.logical_and, checks)

    def device(d):
        return (gx + DIRS[d][0], gy + DIRS[d][1])

    box = (pl.ds(PX, NX), pl.ds(PY, NY))

    def load(i):
        pairs = [(ids_in, ids.at[pl.ds(PX, NX), pl.ds(8, NY)])]
        for comp in range(3):
            pairs.append((e_in.at[comp], et.at[(comp, *box)]))
            pairs.append((m_in.at[comp], ht.at[(comp, *box)]))
        return pltpu.make_async_copy(*pairs[i], local.at[i])

    for i in range(7):
        load(i).start()
    def clear_pieces(slot, c):
        for d in range(8):
            mid, tiles = MID[d], TILES[d]
            inn[d][slot, pl.ds(mid, tiles - mid)] = jnp.zeros((tiles - mid, 8, NZ), jnp.float32)
        return c

    lax.fori_loop(0, SLOTS, clear_pieces, 0)
    barrier = pltpu.get_barrier_semaphore()
    for d in range(8):
        @pl.when(there(d))
        def _(d=d):
            pl.semaphore_signal(barrier, inc=1, device_id=device(d), device_id_type=MESH)
    def around(d):
        dx, dy = DIRS[d]
        xd = pl.ds(PX + NX if dx < 0 else PX - IDS, IDS) if dx else pl.ds(PX, NX)
        yd = pl.ds(8 + NY if dy < 0 else 8 - IDS, IDS) if dy else pl.ds(8, NY)
        return xd, yd

    def id_copy(d):
        xd, yd = around(d)
        dx, dy = DIRS[d]
        xs = pl.ds(0 if dx < 0 else NX - IDS, IDS) if dx else pl.ds(0, NX)
        ys = pl.ds(0 if dy < 0 else NY - IDS, IDS) if dy else pl.ds(0, NY)
        return pltpu.make_async_remote_copy(
            src_ref=ids_in.at[xs, ys],
            dst_ref=ids.at[xd, yd],
            send_sem=out_sem.at[d],
            recv_sem=id_in.at[d],
            device_id=device(d),
            device_id_type=MESH,
        )

    for d in range(8):
        @pl.when(jnp.logical_not(there(OPPOSITE[d])))
        def _(d=d):
            xd, yd = around(d)
            ids[xd, yd] = jnp.full((xd.size, yd.size, NZ), -1, jnp.int32)

            if MID[d]:
                def clear(s, c):
                    inn[d][s, pl.ds(0, MID[d])] = jnp.zeros((MID[d], 8, NZ), jnp.float32)
                    return c

                lax.fori_loop(0, SLOTS, clear, 0)

    def clear_planes(x, c):
        for comp in range(3):
            jj[comp, x] = jnp.zeros((YP - 16, NZ), jnp.float32)
            for a in (ef, hf):
                a[comp, x] = jnp.zeros((YP, NZ), jnp.float32)
        return c

    lax.fori_loop(0, XP, clear_planes, 0)
    for step in range(STEPS):
        amps[step] = np.float32(np.sin(np.float32(0.3 * (step + 1))))

    def parts_h(d, depth):
        mid, pieces = MID[d], []
        before, less = pl.ds(DEEP - depth, depth), pl.ds(0, depth - 1)
        if d in (E, N):
            pieces.append((pl.ds(0, mid), pl.ds(0, 8)))
        if d in (W, S, NW, SE):
            pieces.append((pl.ds(mid, 2), before))
        if d in (E, N, NE) and depth > 1:
            pieces.append((pl.ds(mid, 4 if d == NE else 2), less))
        return pieces

    def parts_e(d, depth):
        mid, pieces = MID[d], []
        before, after = pl.ds(DEEP - depth, depth), pl.ds(0, depth)
        if d in (W, S):
            pieces.append((pl.ds(0, mid), pl.ds(0, 8)))
        if depth and d != NE:
            pieces.append((pl.ds(0, 4) if d == SW else pl.ds(mid + 2, 2), before if d in (W, S, SW) else after))
        return pieces

    def parts(d, depth, last):
        return (parts_h(d, depth) if depth else []) + ([] if last else parts_e(d, depth))

    def rows_of(d, depth, last):
        return sum(ts.size * rows.size for ts, rows in parts(d, depth, last))

    def turn(block, depth):
        return lax.rem(block, 2) * (BLOCK + 1) + depth

    def start(block, slot, depth, some):
        for d in (N, S, W, E, NW, NE, SW, SE):
            if some(d, depth):
                @pl.when(there(d))
                def _(d=d):
                    for ts, rows in some(d, depth):
                        pltpu.make_async_remote_copy(
                            src_ref=out[d].at[slot, ts, rows],
                            dst_ref=inn[d].at[slot, ts, rows],
                            send_sem=out_sem.at[d],
                            recv_sem=in_sem.at[d, turn(block, depth)],
                            device_id=device(d),
                            device_id_type=MESH,
                        ).start()

    def all_of(rows, sem):
        some = total.at[pl.ds(0, rows)]
        return pltpu.make_async_copy(some, some, sem)

    def arrive(block, slot, depth, last):
        for d in range(8):
            if parts(d, depth, last):
                @pl.when(there(OPPOSITE[d]))
                def _(d=d):
                    all_of(rows_of(d, depth, last), in_sem.at[d, turn(block, depth)]).wait()

    def leave():
        for d in range(8):
            @pl.when(there(d))
            def _(d=d):
                rows = (IDS if DIRS[d][0] else NX) * (IDS if DIRS[d][1] else NY)
                for size in SIZES:
                    rows += sum(rows_of(d, m, m == size) for m in range(size + 1))
                all_of(rows, out_sem.at[d]).wait()

    def one_of(depths, do, block, slot, depth, *what):
        for m in depths:
            @pl.when(depth == m)
            def _(m=m):
                do(block, slot, m, *what)

    XA, XZ, YA, YZ = PX, PX + NX - 1, PY, PY + NY - 1

    def put_face(d, slot, at, a, comps, x):
        for i, c in enumerate(comps):
            out[d][slot, pl.ds(at + 4 * i, 4)] = a[c, x, pl.ds(YA, NY)].reshape(4, 8, NZ)

    def put_line(d, slot, at, a, comps, y):
        for i, c in enumerate(comps):
            out[d][slot, pl.ds(at + 2 * i, 2)] = a[c, pl.ds(XA, NX), y].reshape(2, 8, NZ)

    def put_piece_y(d, slot, at, a, x, top):
        for i, c in enumerate((1, 2)):
            out[d][slot, at + i] = a[c, x, pl.ds(YZ + 1 if top else YA - DEEP, 8)]

    def put_piece_x(d, slot, at, a, y, right):
        for i, c in enumerate((0, 2)):
            out[d][slot, at + i, pl.ds(0, DEEP)] = a[c, pl.ds(XZ + 1 if right else XA - DEEP, DEEP), y]

    def pack_first(slot):
        put_face(W, slot, 0, et, (1, 2), XA)
        put_line(S, slot, 0, et, (0, 2), YA)
        own_x[slot, pl.ds(2, 2)] = jnp.zeros((2, NY, NZ), jnp.float32)
        own_y[slot, pl.ds(2, 2)] = jnp.zeros((2, NX, NZ), jnp.float32)

    def pack_e(slot):
        put_face(W, slot, 0, ef, (1, 2), XA)
        put_line(S, slot, 0, ef, (0, 2), YA)
        for i, c in enumerate((1, 2)):
            own_x[slot, 2 + i] = ef[c, XZ + 1, pl.ds(YA, NY)]
        for i, c in enumerate((0, 2)):
            own_y[slot, 2 + i] = ef[c, pl.ds(XA, NX), YZ + 1]
        put_piece_x(W, slot, 10, ef, YZ + 1, False)
        put_piece_x(E, slot, 10, ef, YZ + 1, True)
        put_piece_y(S, slot, 6, ef, XZ + 1, False)
        put_piece_y(N, slot, 6, ef, XZ + 1, True)
        put_piece_y(NW, slot, 2, ef, XA, True)
        put_piece_y(SW, slot, 0, ef, XA, False)
        put_piece_x(SW, slot, 2, ef, YA, False)
        put_piece_x(SE, slot, 2, ef, YA, True)

    def pack_h(slot):
        put_face(E, slot, 0, hf, (1, 2), XZ)
        put_line(N, slot, 0, hf, (0, 2), YZ)
        for i, c in enumerate((1, 2)):
            own_x[slot, i] = hf[c, XA - 1, pl.ds(YA, NY)]
        for i, c in enumerate((0, 2)):
            own_y[slot, i] = hf[c, pl.ds(XA, NX), YA - 1]
        put_piece_x(W, slot, 8, hf, YA - 1, False)
        put_piece_x(E, slot, 8, hf, YA - 1, True)
        put_piece_y(S, slot, 4, hf, XA - 1, False)
        put_piece_y(N, slot, 4, hf, XA - 1, True)
        put_piece_x(NW, slot, 0, hf, YZ, False)
        put_piece_y(NE, slot, 0, hf, XZ, True)
        put_piece_x(NE, slot, 2, hf, YZ, True)
        put_piece_y(SE, slot, 0, hf, XZ, False)

    def ring_x(a, x, slot, own, face, low, high):
        for i, c in enumerate((1, 2)):
            d, at = face
            a[c, x, pl.ds(YA, NY)] = own_x[slot, own + i] + inn[d][slot, pl.ds(at + 4 * i, 4)].reshape(NY, NZ)
            for pieces, row in ((low, YA), (high, YA + NY - DEEP)):
                (d1, at1), (d2, at2) = pieces
                some = pl.ds(0, DEEP)
                a[c, x, pl.ds(row, DEEP)] += inn[d1][slot, at1 + i, some] + inn[d2][slot, at2 + i, some]

    def ring_y(a, y, slot, own, face, low, high):
        for i, c in enumerate((0, 2)):
            d, at = face
            ring[...] = own_y[slot, own + i] + inn[d][slot, pl.ds(at + 2 * i, 2)].reshape(NX, NZ)
            for pieces, row in ((low, 0), (high, NX - DEEP)):
                (d1, at1), (d2, at2) = pieces
                some = pl.ds(0, DEEP)
                ring[pl.ds(row, DEEP)] += inn[d1][slot, at1 + i, some] + inn[d2][slot, at2 + i, some]
            a[c, pl.ds(XA, NX), y] = ring[...]

    def ring_e(slot):
        ring_x(et, XZ + 1, slot, 2, (W, 0), ((N, 6), (NW, 2)), ((S, 6), (SW, 0)))
        ring_y(et, YZ + 1, slot, 2, (S, 0), ((E, 10), (SE, 2)), ((W, 10), (SW, 2)))

    def ring_h(slot):
        ring_x(ht, XA - 1, slot, 0, (E, 0), ((N, 4), (NE, 0)), ((S, 4), (SE, 0)))
        ring_y(ht, YA - 1, slot, 0, (N, 0), ((E, 8), (NE, 2)), ((W, 8), (NW, 0)))

    def look(x, planes, row, n, source):
        xs, rows = pl.ds(x, planes), pl.ds(row, n)
        here = ids[xs, rows]
        bits = [(here & (1 << b)) != 0 for b in range(3)]
        real = here >= 0

        def pick(c):
            level = [table[m, c] for m in range(MATS)]
            for b in range(3):
                level = [jnp.where(bits[b], level[2 * i + 1], level[2 * i]) for i in range(len(level) // 2)]
            return level[0]

        tensor = [jnp.where(real, 0.45 * pick(c), 0.0) for c in range(6)]
        for c in range(6):
            kk[c, xs, rows] = tensor[c]
        if source:
            xx, yy, zz, xy, xz, yz = tensor
            s0, s1, s2 = (pick(c) for c in (6, 7, 8))
            jj[0, xs, rows] = xx * s0 + xy * s1 + xz * s2
            jj[1, xs, rows] = xy * s0 + yy * s1 + yz * s2
            jj[2, xs, rows] = xz * s0 + yz * s1 + zz * s2

    def look_own(i, c):
        look(PX + 2 * i, 2, 8, NY, True)
        return c

    def look_rows(i, c):
        look(PX + 4 * i, 4, 0, 8, False)
        look(PX + 4 * i, 4, 8 + NY, 8, False)
        return c

    def look_planes(i, c):
        look(PX - IDS + i, 1, 0, NY + 16, False)
        look(PX + NX + i, 1, 0, NY + 16, False)
        return c

    def frame(update):
        wide, halo = BLOCK - 1, BLOCK // 2
        update(PX - wide, NX + 2 * wide, 8, 16)
        update(PX - wide, NX + 2 * wide, 40, 16)
        update(PX - halo - 1, halo + BLOCK, 24, 16)
        update(PX + NX - BLOCK, halo + BLOCK, 24, 16)

    def lines_h(update):
        update(PX - BLOCK, NX + 2 * BLOCK, 8, 8)
        update(PX - BLOCK, NX + 2 * BLOCK, 40, 8)
        for x in (PX - 1, PX + NX - 1):
            update(x, 1, 16, 24)
            update(x, 1, 48, 8)

    def copy_in(i, c):
        xs, rows = pl.ds(PX + 4 * i, 4), pl.ds(PY, NY)
        for comp in range(3):
            for a, t in ((ef, et), (hf, ht)):
                a[comp, xs, rows] = t[comp, xs, rows]
        return c

    def clean_rows(i, c):
        for comp in range(3):
            for a in (ef, hf):
                for row in (8, PY + NY):
                    a[comp, pl.ds(PX + 4 * i, 4), pl.ds(row, 8)] = jnp.zeros((4, 8, NZ), jnp.float32)
        return c

    def clean_plane(x, c):
        for comp in range(3):
            for a in (ef, hf):
                for at in (x, x + PX + NX):
                    a[comp, at, pl.ds(8, NY + 16)] = jnp.zeros((NY + 16, NZ), jnp.float32)
        return c

    def clean():
        lax.fori_loop(0, NX // 4, clean_rows, 0)
        lax.fori_loop(0, PX, clean_plane, 0)

    def edges_h():
        @pl.when(gx == 0)
        def _():
            for comp in range(3):
                hf[comp, PX - 1, pl.ds(8, NY + 16)] = jnp.zeros((NY + 16, NZ), jnp.float32)

        @pl.when(gy == 0)
        def _():
            for comp in range(3):
                hf[comp, :, pl.ds(8, 8)] = jnp.zeros((XP, 8, NZ), jnp.float32)

    def true_step(step, slot, wait, early=lambda: None):
        some_e = functools.partial(update_e, et, ht, kk, jj, amps[step])
        ring_e(slot - 1)
        update_h(et, ht, PX, NX, PY, NY)
        some_e(PX + 1, NX - 1, PY + 8, NY - 8)
        early()
        wait()
        ring_h(slot)
        some_e(PX, 1, PY, NY)
        some_e(PX + 1, NX - 1, PY, 8)

    def stores():
        pairs = [(a.at[(comp, *box)], o.at[comp]) for a, o in ((et, e_out), (ht, m_out)) for comp in range(3)]
        return [pltpu.make_async_copy(src, dst, local.at[1 + i]) for i, (src, dst) in enumerate(pairs)]

    load(0).wait()
    lax.fori_loop(0, NX // 2, look_own, 0)
    for i in range(1, 7):
        load(i).wait()
    lax.fori_loop(0, NX // 4, copy_in, 0)
    pack_first(0)
    lines_h(functools.partial(update_h, ef, hf))
    edges_h()
    pack_h(1)
    peers = sum(there(d).astype(jnp.int32) for d in range(8))
    pl.semaphore_wait(barrier, peers)
    start(0, 0, 0, parts_e)
    start(0, 1, 1, parts_h)
    for d in (N, S, W, E, NW, NE, SW, SE):
        @pl.when(there(d))
        def _(d=d):
            id_copy(d).start()
    clean()
    arrive(0, 0, 0, False)
    true_step(0, 1, functools.partial(arrive, 0, 1, 1, True))
    def look_around():
        for d in range(8):
            @pl.when(there(OPPOSITE[d]))
            def _(d=d):
                id_copy(d).wait_recv()
        lax.fori_loop(0, NX // 4, look_rows, 0)
        lax.fori_loop(0, IDS, look_planes, 0)

    def block(b, c):
        first = lax.div(1, b)
        size, begin, base = 4 - first, 4 * b - 4 + first, 5 * b - 4 + first
        pack_first(base)
        start(b, base, 0, parts_e)
        lax.fori_loop(0, NX // 4, copy_in, 0)

        def free(t, c):
            frame(functools.partial(update_h, ef, hf))
            edges_h()
            pack_h(base + t)
            one_of(range(1, BLOCK), start, b, base + t, t, parts_h)

            @pl.when((b == 1) & (t == 1))
            def _():
                look_around()

            frame(functools.partial(update_e, ef, hf, kk, jj, amps[begin + t - 1]))
            pack_e(base + t)
            one_of(range(1, BLOCK), start, b, base + t, t, parts_e)
            return c

        lax.fori_loop(1, size, free, 0)
        lines_h(functools.partial(update_h, ef, hf))
        edges_h()
        pack_h(base + size)
        one_of((BLOCK - 1, BLOCK), start, b, base + size, size, parts_h)
        clean()
        arrive(b, base, 0, False)

        def true(t, c):
            def wait():
                @pl.when(t < size)
                def _():
                    one_of(range(1, BLOCK), arrive, b, base + t, t, False)

                @pl.when(t == size)
                def _():
                    one_of((BLOCK - 1, BLOCK), arrive, b, base + t, t, True)

            def early():
                @pl.when(begin + t == STEPS)
                def _():
                    for copy in stores()[3:]:
                        copy.start()

            true_step(begin + t - 1, base + t, wait, early)
            return c

        lax.fori_loop(1, size + 1, true, 0)
        return c

    lax.fori_loop(1, 4, block, 0)

    for copy in stores()[:3]:
        copy.start()


    leave()
    for copy in stores():
        copy.wait()


def hand_over(e_in, m_in, e_out, m_out, held, in_sem, out_sem):
    pairs = [(a.at[c], o.at[c]) for a, o in ((e_in, e_out), (m_in, m_out)) for c in range(3)]
    loads = [pltpu.make_async_copy(a, held.at[i], in_sem.at[i]) for i, (a, _) in enumerate(pairs)]
    stores = [pltpu.make_async_copy(held.at[i], o, out_sem.at[i]) for i, (_, o) in enumerate(pairs)]
    for load in loads:
        load.start()
    for load, store in zip(loads, stores):
        load.wait()
        store.start()
    for store in stores:
        store.wait()


def shards(electric, magnetic, material_ids, material_table):
    field = jax.ShapeDtypeStruct((3, NX, NY, NZ), jnp.float32)
    hbm = pl.BlockSpec(memory_space=pl.ANY)
    big = pltpu.VMEM((3, XP, YP, NZ), jnp.float32)
    messages = [pltpu.VMEM((SLOTS, TILES[d], 8, NZ), jnp.float32) for d in range(8)]
    e, m = pl.pallas_call(
        kernel,
        out_shape=(field, field),
        in_specs=[hbm, hbm, hbm, pl.BlockSpec(memory_space=pltpu.SMEM)],
        out_specs=(hbm, hbm),
        scratch_shapes=[
            big,
            big,
            big,
            big,
            pltpu.VMEM((6, XP, YP - 16, NZ), jnp.float32),
            pltpu.VMEM((3, XP, YP - 16, NZ), jnp.float32),
            pltpu.VMEM((XP, YP - 16, NZ), jnp.int32),
            pltpu.VMEM((SLOTS, 4, NY, NZ), jnp.float32),
            pltpu.VMEM((SLOTS, 4, NX, NZ), jnp.float32),
            pltpu.VMEM((NX, NZ), jnp.float32),
            pltpu.VMEM((2048, NZ), jnp.float32),
            pltpu.SMEM((STEPS,), jnp.float32),
            *messages,
            *messages,
            pltpu.SemaphoreType.DMA((8,)),
            pltpu.SemaphoreType.DMA((8, TURNS)),
            pltpu.SemaphoreType.DMA((8,)),
            pltpu.SemaphoreType.DMA((7,)),
        ],
        compiler_params=pltpu.CompilerParams(
            collective_id=0, has_side_effects=True, vmem_limit_bytes=56 * 1024 * 1024
        ),
    )(electric, magnetic, material_ids, material_table)
    return pl.pallas_call(
        hand_over,
        out_shape=(field, field),
        in_specs=[hbm, hbm],
        out_specs=(hbm, hbm),
        scratch_shapes=[pltpu.VMEM((6, NX, NY, NZ), jnp.float32), pltpu.SemaphoreType.DMA((6,)), pltpu.SemaphoreType.DMA((6,))],
    )(e, m)


def solution(mesh):
    placed = (P(None, "gx", "gy", None), P(None, "gx", "gy", None), P("gx", "gy", None), P())
    return jax.shard_map(
        shards,
        mesh=mesh,
        in_specs=placed,
        out_specs=(P(None, "gx", "gy", None), P(None, "gx", "gy", None)),
        check_vma=False,
    )
```
